32 devices in a mesh: fsdp: 32 (over z, y, x, core).
Axes of the slice: x: 2, y: 2, z: 4, core: 2. Of those that a mesh axis runs over, the one named last changes fastest.
Arguments:
- tokens: bfloat16 [8192, 576], P('fsdp'), may hold values from -6 to 6
- segments: int32 [32, 256], P('fsdp'), may hold values from 0 to 2, never falling along the last dimension, each value on 1 to 128 neighbouring positions
- cotangent: bfloat16 [8192, 576], P('fsdp'), may hold values from -18 to 18
- norm_gains: float32 [2, 576], replicated, may hold values from 0.25 to 1.75
- w_query: bfloat16 [331776], P('fsdp'), may hold values from -0.25 to 0.25
- w_key: bfloat16 [110592], P('fsdp'), may hold values from -0.25 to 0.25
- w_value: bfloat16 [110592], P('fsdp'), may hold values from -0.25 to 0.25
- w_output: bfloat16 [331776], P('fsdp'), may hold values from -1.5 to 1.5
- w_gate: bfloat16 [884736], P('fsdp'), may hold values from -0.25 to 0.25
- w_up: bfloat16 [884736], P('fsdp'), may hold values from -0.25 to 0.25
- w_down: bfloat16 [884736], P('fsdp'), may hold values from -0.21875 to 0.21875
Outputs:
- output: bfloat16 [8192, 576], P('fsdp')
- input_grad: bfloat16 [8192, 576], P('fsdp')
- gain_grads: float32 [2, 576], replicated
- query_grad: float32 [331776], P('fsdp')
- key_grad: float32 [110592], P('fsdp')
- value_grad: float32 [110592], P('fsdp')
- output_grad: float32 [331776], P('fsdp')
- gate_grad: float32 [884736], P('fsdp')
- up_grad: float32 [884736], P('fsdp')
- down_grad: float32 [884736], P('fsdp')
The draws below stay inside these ranges and needn't reach their ends.
Inputs may be any that keep to these rules, and one draw needn't show every extreme that they name: `segments`: document numbers never fall along a sequence; each of the 3 documents has one token or more, and in every sequence the longest has exactly 128 tokens.
All inputs are finite; a program needn't handle non-finite values.
Results may differ from the reference program's by a relative error of at most 0.013.
Values may be sent and summed in bfloat16 or wider, within the bound.
A program may use at most 128 MiB of HBM per device.

```python
import math
import jax
import jax.numpy as jnp
import numpy as np
from jax import lax

D = 576
FF = 1536
HEADS = 9
KV_HEADS = 3
HEAD_DIM = 64
TOK_DEV = 256
DOCS = 3
SEQS = 32
TOKENS = 8192


def draw_cotangent(key, part):
    key = jax.random.fold_in(key, 7)
    position = (jnp.arange(TOKENS, dtype=jnp.float32) / (TOKENS - 1))[:, None]
    sample = jnp.clip(jax.random.normal(key, (TOKENS, D), jnp.float32), -6.0, 6.0)
    result = sample * (1.0 + 2.0 * position)
    return result.astype(jnp.bfloat16)


def level_of(rng, dims, cuts, smallest, high):
    loudness, own = 1.0, jax.random.fold_in(rng, 6)
    for dim, parts in cuts:
        draws = jnp.exp(jax.random.uniform(jax.random.fold_in(own, dim), (parts,), jnp.float32, smallest / len(cuts), high / len(cuts)))
        loudness = loudness * jnp.repeat(draws, dims[dim] // parts).reshape([-1 if axis == dim else 1 for axis in range(len(dims))])
    return loudness


def length_profile(amount, total, reach, slope):
    weights = [(1 << 20) // math.isqrt(standing ** slope) + 1 for standing in range(2, amount + 1)]
    surplus, counts = total - reach - (amount - 1), [1] * (amount - 1)
    while surplus > 0:
        free = [i for i in range(amount - 1) if counts[i] < reach]
        mass, remaining = sum([weights[i] for i in free]), surplus
        for i in free:
            extra = min(reach - counts[i], max(1, remaining * weights[i] // mass), surplus)
            counts[i] = counts[i] + extra
            surplus = surplus - extra
    return np.array([reach] + counts)


def ragged(stream_key, count, total, reach, lean):
    if count == 2:
        one = jax.random.randint(stream_key, (), max(1, total - reach), min(reach, total - 1) + 1)
        return jnp.stack([one, total - one])
    tallies = jnp.asarray(length_profile(count, total, reach, lean), jnp.int32)
    couples = (count - 1) // 2
    source_of, receiver = tallies[1:1 + 2 * couples:2], tallies[2:2 + 2 * couples:2]
    slack = jnp.minimum(source_of - 1, reach - receiver)
    moved = jax.random.randint(jax.random.fold_in(stream_key, 1), (couples,), 0, 1 << 20) % (slack + 1)
    tallies = tallies.at[1:1 + 2 * couples:2].set(source_of - moved).at[2:2 + 2 * couples:2].set(receiver + moved)
    return tallies[jax.random.permutation(jax.random.fold_in(stream_key, 2), count)]


def bell_draw(stream_key, dims, scale, most, shards=(), kind=jnp.bfloat16):
    values = scale * jax.random.normal(stream_key, dims, jnp.float32)
    if shards:
        values = values * level_of(stream_key, dims, shards, -0.22, 0.18)
    return jnp.clip(values, -most, most).astype(kind)


def setup_inputs(seed: int = 0) -> dict:
    key_of = jax.random.split(jax.random.key(seed), 12)
    return {
        "tokens": bell_draw(key_of[0], (TOKENS, D), 1.0, 6.0, ((0, 32),)),
        "segments": jax.vmap(lambda own: jnp.searchsorted(jnp.cumsum(ragged(own, DOCS, TOK_DEV, TOK_DEV // 2, 0)), jnp.arange(TOK_DEV), side="right"))(jax.random.split(key_of[1], SEQS)).reshape((SEQS, TOK_DEV)).astype(jnp.int32),
        "cotangent": draw_cotangent(jax.random.fold_in(key_of[11], 71), 0),
        "norm_gains": jnp.clip(1.0 + 0.15 * jax.random.normal(key_of[3], (2, D), jnp.float32), 0.25, 1.75),
        "w_query": bell_draw(key_of[4], (D * D,), D ** -0.5, 0.25, ((0, 32),)),
        "w_key": bell_draw(key_of[5], (D * KV_HEADS * HEAD_DIM,), D ** -0.5, 0.25, ((0, 32),)),
        "w_value": bell_draw(key_of[6], (D * KV_HEADS * HEAD_DIM,), D ** -0.5, 0.25, ((0, 32),)),
        "w_output": bell_draw(key_of[7], (D * D,), (max(D // 32, 1)) ** -0.5, 1.5, ((0, 32),)),
        "w_gate": bell_draw(key_of[8], (D * FF,), D ** -0.5, 0.25, ((0, 32),)),
        "w_up": bell_draw(key_of[9], (D * FF,), D ** -0.5, 0.25, ((0, 32),)),
        "w_down": bell_draw(key_of[10], (FF * D,), (FF // 2) ** -0.5, 0.21875, ((0, 32),)),
    }


EPSILON = 1e-05
THETA = 100000.0
NEGATIVE = -1e+30

@jax.custom_vjp
def low(v):
    return lax.optimization_barrier(v.astype(jnp.bfloat16)).astype(jnp.float32)

@jax.custom_vjp
def low_back(v):
    return v

def low_keep(v):
    return (low(v), None)

def low_pass(kept, grad):
    return (grad,)

def back_keep(v):
    return (v, None)

def back_low(kept, grad):
    return (low(grad),)
low.defvjp(low_keep, low_pass)
low_back.defvjp(back_keep, back_low)

def rotary_tables(segment_row):
    length = segment_row.shape[0]
    positions = jnp.arange(length, dtype=jnp.int32)
    doc_ids = jnp.arange(DOCS, dtype=jnp.int32)
    starts = lax.optimization_barrier(jnp.sum((segment_row[None, :] < doc_ids[:, None]).astype(jnp.int32), axis=1))
    member = (segment_row[:, None] == doc_ids[None, :]).astype(jnp.int32)
    offsets = positions - lax.optimization_barrier(jnp.sum(member * starts[None, :], axis=1))
    frequency = jnp.exp(jnp.arange(0, HEAD_DIM, 2).astype(jnp.float32) * (-math.log(THETA) / HEAD_DIM))
    angles = offsets.astype(jnp.float32)[:, None] * frequency[None, :]
    angles = jnp.concatenate([angles, angles], axis=1)
    return (jnp.cos(angles), jnp.sin(angles))

def rotate_pairs(vectors, cosine_table, sine_table):
    half_width = vectors.shape[-1] // 2
    turned = jnp.concatenate([-vectors[..., half_width:], vectors[..., :half_width]], axis=-1)
    return vectors * cosine_table[:, None, :] + turned * sine_table[:, None, :]

def matmul_high(first, second):
    return jnp.dot(first, second, precision=lax.Precision.HIGHEST, preferred_element_type=jnp.float32)

def forward(inputs, gain_rows, mat_query, mat_key, mat_value, mat_output, mat_gate, mat_up, mat_down, cosine_table, sine_table, allowed):
    row_count = inputs.shape[0]
    group_size = HEADS // KV_HEADS
    score_scale = HEAD_DIM ** (-0.5)
    inverse_one = lax.rsqrt(lax.optimization_barrier(jnp.mean(inputs * inputs, axis=-1, keepdims=True)) + EPSILON)
    normed_one = low(inputs * inverse_one * gain_rows[0])
    queries = low_back(matmul_high(normed_one, mat_query)).reshape(row_count, HEADS, HEAD_DIM)
    key_rows = low_back(matmul_high(normed_one, mat_key)).reshape(row_count, KV_HEADS, HEAD_DIM)
    value_rows = low_back(matmul_high(normed_one, mat_value)).reshape(row_count, KV_HEADS, HEAD_DIM)
    queries = low(rotate_pairs(queries, cosine_table, sine_table)).reshape(row_count, KV_HEADS, group_size, HEAD_DIM)
    key_rows = low(rotate_pairs(key_rows, cosine_table, sine_table))
    value_rows = low(value_rows)
    scores = low_back(jnp.einsum('qkgd,tkd->kgqt', queries, key_rows, precision=lax.Precision.HIGHEST) * score_scale)
    scores = jnp.where(allowed[None, None], scores, NEGATIVE)
    attention = jax.nn.softmax(scores, axis=-1)
    mixed = jnp.einsum('kgqt,tkd->qkgd', low(attention), value_rows, precision=lax.Precision.HIGHEST).reshape(row_count, D)
    mixed = low(low_back(mixed))
    residual = inputs + low_back(matmul_high(mixed, mat_output))
    inverse_two = lax.rsqrt(lax.optimization_barrier(jnp.mean(residual * residual, axis=-1, keepdims=True)) + EPSILON)
    normed_two = low(residual * inverse_two * gain_rows[1])
    gate_pre = low_back(matmul_high(normed_two, mat_gate))
    up_pre = low_back(matmul_high(normed_two, mat_up))
    hidden = low(jax.nn.silu(gate_pre) * up_pre)
    return residual + low_back(matmul_high(hidden, mat_down))

def reference(tokens, segments, cotangent, norm_gains, w_query, w_key, w_value, w_output, w_gate, w_up, w_down):
    width_kv = KV_HEADS * HEAD_DIM
    matrices = (w_query.astype(jnp.float32).reshape(D, D), w_key.astype(jnp.float32).reshape(D, width_kv), w_value.astype(jnp.float32).reshape(D, width_kv), w_output.astype(jnp.float32).reshape(D, D), w_gate.astype(jnp.float32).reshape(D, FF), w_up.astype(jnp.float32).reshape(D, FF), w_down.astype(jnp.float32).reshape(FF, D))
    seq_count = segments.shape[0]
    row_count = segments.shape[1]
    input_seqs = tokens.astype(jnp.float32).reshape(seq_count, row_count, D)
    cot_seqs = cotangent.astype(jnp.float32).reshape(seq_count, row_count, D)
    gain_rows = norm_gains.astype(jnp.float32)

    def step(grad_sums, sequence_item):
        inputs, segment_row, cot_rows = sequence_item
        cosine_table, sine_table = rotary_tables(segment_row)
        positions = jnp.arange(row_count, dtype=jnp.int32)
        allowed = (positions[None, :] <= positions[:, None]) & (segment_row[None, :] == segment_row[:, None])

        def layer_fn(input_rows, gain_values, *weight_mats):
            return forward(input_rows, gain_values, *weight_mats, cosine_table, sine_table, allowed)
        layer_out, pullback = jax.vjp(layer_fn, inputs, gain_rows, *matrices)
        gradients = pullback(cot_rows)
        grad_sums = tuple((first + second for first, second in zip(grad_sums, gradients[1:])))
        return (grad_sums, (layer_out.astype(jnp.bfloat16), gradients[0].astype(jnp.bfloat16)))
    zero_sums = (jnp.zeros_like(gain_rows),) + tuple((jnp.zeros_like(matrix) for matrix in matrices))
    grad_sums, (layer_outs, input_grads) = lax.scan(step, zero_sums, (input_seqs, segments, cot_seqs))
    return (layer_outs.reshape(-1, D), input_grads.reshape(-1, D), grad_sums[0], grad_sums[1].reshape(-1), grad_sums[2].reshape(-1), grad_sums[3].reshape(-1), grad_sums[4].reshape(-1), grad_sums[5].reshape(-1), grad_sums[6].reshape(-1), grad_sums[7].reshape(-1))
```

```python
import functools
import math

import jax
import jax.numpy as jnp
from jax import lax
from jax.experimental import pallas as pl
from jax.experimental.pallas import tpu as pltpu
from jax.sharding import PartitionSpec as P

D = 576
FF = 1536
HEADS = 9
KV_HEADS = 3
HEAD_DIM = 64
DOCS = 3


EPSILON = 1e-05
THETA = 100000.0
NEGATIVE = -1e30


def rotary_tables(segment_row):
    length = segment_row.shape[0]
    positions = jnp.arange(length, dtype=jnp.int32)
    doc_ids = jnp.arange(DOCS, dtype=jnp.int32)
    starts = jnp.sum((segment_row[None, :] < doc_ids[:, None]).astype(jnp.int32), axis=1)
    member = (segment_row[:, None] == doc_ids[None, :]).astype(jnp.int32)
    offsets = positions - jnp.sum(member * starts[None, :], axis=1)
    frequency = jnp.exp(
        jnp.arange(0, HEAD_DIM, 2).astype(jnp.float32) * (-math.log(THETA) / HEAD_DIM)
    )
    angles = offsets.astype(jnp.float32)[:, None] * frequency[None, :]
    angles = jnp.concatenate([angles, angles], axis=1)
    return (jnp.cos(angles), jnp.sin(angles))


def rotate_pairs(vectors, cosine_table, sine_table):
    half_width = vectors.shape[-1] // 2
    turned = jnp.concatenate([-vectors[..., half_width:], vectors[..., :half_width]], axis=-1)
    return vectors * cosine_table[:, None, :] + turned * sine_table[:, None, :]


def rotate_back(gradient, cosine_table, sine_table):
    half_width = gradient.shape[-1] // 2
    scaled = gradient * sine_table[:, None, :]
    turned = jnp.concatenate([scaled[..., half_width:], -scaled[..., :half_width]], axis=-1)
    return gradient * cosine_table[:, None, :] + turned


def norm_forward(vectors, gain_row):
    inverse = lax.rsqrt(jnp.mean(vectors * vectors, axis=-1, keepdims=True) + EPSILON)
    unit_rows = vectors * inverse
    return (unit_rows * gain_row, unit_rows, inverse)


def norm_backward(upstream, unit_rows, inverse, gain_row):
    scaled = upstream * gain_row
    grad_in = inverse * (scaled - unit_rows * jnp.mean(scaled * unit_rows, axis=-1, keepdims=True))
    return (grad_in, jnp.sum(upstream * unit_rows, axis=0))


def left_dot(first, second):
    return lax.dot_general(
        first, second, (((0,), (0,)), ((), ())), preferred_element_type=jnp.float32
    )


def right_dot(first, second):
    return lax.dot_general(
        first, second, (((1,), (1,)), ((), ())), preferred_element_type=jnp.float32
    )


def attn_shapes(flat_list):
    width_kv = KV_HEADS * HEAD_DIM
    return (
        flat_list[0].reshape(D, D),
        flat_list[1].reshape(D, width_kv),
        flat_list[2].reshape(D, width_kv),
        flat_list[3].reshape(D, D),
    )


def mlp_shapes(flat_list):
    return (flat_list[0].reshape(D, FF), flat_list[1].reshape(D, FF), flat_list[2].reshape(FF, D))


def plain_body(
    tokens, segments, cotangent, norm_gains, w_query, w_key, w_value, w_output, w_gate, w_up, w_down
):
    row_count = tokens.shape[0]
    width_kv = KV_HEADS * HEAD_DIM
    group_size = HEADS // KV_HEADS
    score_scale = HEAD_DIM ** (-0.5)
    block_rows = min(512, row_count)
    segment_row = segments[0]
    cosine_table, sine_table = rotary_tables(segment_row)
    inputs = tokens.astype(jnp.float32)
    attn_flat = (
        lax.all_gather(w_query, "fsdp", axis=0, tiled=True),
        lax.all_gather(w_key, "fsdp", axis=0, tiled=True),
        lax.all_gather(w_value, "fsdp", axis=0, tiled=True),
        lax.all_gather(w_output, "fsdp", axis=0, tiled=True),
    )
    mat_query, mat_key, mat_value, mat_output = attn_shapes(attn_flat)
    normed_one, unit_one, inverse_one = norm_forward(inputs, norm_gains[0])
    normed_one = normed_one.astype(jnp.bfloat16)
    queries = jnp.dot(normed_one, mat_query, preferred_element_type=jnp.float32).reshape(
        row_count, HEADS, HEAD_DIM
    )
    key_rows = jnp.dot(normed_one, mat_key, preferred_element_type=jnp.float32).reshape(
        row_count, KV_HEADS, HEAD_DIM
    )
    value_rows = jnp.dot(normed_one, mat_value, preferred_element_type=jnp.float32).astype(
        jnp.bfloat16
    )
    value_rows = value_rows.reshape(row_count, KV_HEADS, HEAD_DIM)
    queries = rotate_pairs(queries, cosine_table, sine_table).astype(jnp.bfloat16)
    queries = queries.reshape(row_count, KV_HEADS, group_size, HEAD_DIM)
    key_rows = rotate_pairs(key_rows, cosine_table, sine_table).astype(jnp.bfloat16)

    def block_scores(block_start, key_end):
        query_pos = block_start + jnp.arange(block_rows)
        key_pos = jnp.arange(key_end)
        causal = key_pos[None, :] <= query_pos[:, None]
        same_doc = segment_row[:, None] == segment_row[None, :]
        scores = (
            jnp.einsum("qkgd,tkd->kgqt", queries, key_rows, preferred_element_type=jnp.float32)
            * score_scale
        )
        return jnp.where((causal & same_doc)[None, None], scores, NEGATIVE)

    block_start = 0
    key_end = block_start + block_rows
    scores = block_scores(block_start, key_end)
    row_peak = jnp.max(scores, axis=-1, keepdims=True)
    exp_scores = jnp.exp(scores - row_peak)
    row_total = jnp.sum(exp_scores, axis=-1, keepdims=True)
    attention = (exp_scores / row_total).astype(jnp.bfloat16)
    logsum_blocks = [row_peak + jnp.log(row_total)]
    mixed_blocks = jnp.einsum(
        "kgqt,tkd->qkgd", attention, value_rows, preferred_element_type=jnp.float32
    )
    mixed = mixed_blocks.reshape(row_count, D).astype(jnp.bfloat16)
    residual = inputs + jnp.dot(mixed, mat_output, preferred_element_type=jnp.float32)
    mlp_flat = (
        lax.all_gather(w_gate, "fsdp", axis=0, tiled=True),
        lax.all_gather(w_up, "fsdp", axis=0, tiled=True),
        lax.all_gather(w_down, "fsdp", axis=0, tiled=True),
    )
    mat_gate, mat_up, mat_down = mlp_shapes(mlp_flat)
    normed_two, unit_two, inverse_two = norm_forward(residual, norm_gains[1])
    normed_two = normed_two.astype(jnp.bfloat16)
    gate_pre = jnp.dot(normed_two, mat_gate, preferred_element_type=jnp.float32)
    up_pre = jnp.dot(normed_two, mat_up, preferred_element_type=jnp.float32)
    activated = jax.nn.silu(gate_pre)
    hidden = (activated * up_pre).astype(jnp.bfloat16)
    output = (residual + jnp.dot(hidden, mat_down, preferred_element_type=jnp.float32)).astype(
        jnp.bfloat16
    )
    mlp_flat = (
        lax.all_gather(w_gate, "fsdp", axis=0, tiled=True),
        lax.all_gather(w_up, "fsdp", axis=0, tiled=True),
        lax.all_gather(w_down, "fsdp", axis=0, tiled=True),
    )
    mat_gate, mat_up, mat_down = mlp_shapes(mlp_flat)
    grad_wdown = left_dot(hidden, cotangent)
    grad_hidden = right_dot(cotangent, mat_down)
    sigmoid_gate = jax.nn.sigmoid(gate_pre)
    grad_gate = (
        grad_hidden * up_pre * sigmoid_gate * (1.0 + gate_pre * (1.0 - sigmoid_gate))
    ).astype(jnp.bfloat16)
    grad_up = (grad_hidden * activated).astype(jnp.bfloat16)
    grad_wgate = left_dot(normed_two, grad_gate)
    grad_wup = left_dot(normed_two, grad_up)
    grad_normed_two = right_dot(grad_gate, mat_gate) + right_dot(grad_up, mat_up)
    grad_from_norm, gain_two = norm_backward(grad_normed_two, unit_two, inverse_two, norm_gains[1])
    grad_residual = cotangent.astype(jnp.float32) + grad_from_norm
    attn_flat = (
        lax.all_gather(w_query, "fsdp", axis=0, tiled=True),
        lax.all_gather(w_key, "fsdp", axis=0, tiled=True),
        lax.all_gather(w_value, "fsdp", axis=0, tiled=True),
        lax.all_gather(w_output, "fsdp", axis=0, tiled=True),
    )
    mat_query, mat_key, mat_value, mat_output = attn_shapes(attn_flat)
    grad_attn = grad_residual.astype(jnp.bfloat16)
    grad_woutput = left_dot(mixed, grad_attn)
    grad_mixed = right_dot(grad_attn, mat_output).astype(jnp.bfloat16)
    grad_mixed = grad_mixed.reshape(row_count, KV_HEADS, group_size, HEAD_DIM)
    grad_query_blocks = []
    grad_keys = jnp.zeros((row_count, KV_HEADS, HEAD_DIM), jnp.float32)
    grad_values = jnp.zeros((row_count, KV_HEADS, HEAD_DIM), jnp.float32)
    for block_index, block_start in enumerate(range(0, row_count, block_rows)):
        key_end = block_start + block_rows
        scores = block_scores(block_start, key_end)
        attention = jnp.exp(scores - logsum_blocks[block_index])
        grad_probs = jnp.einsum(
            "qkgd,tkd->kgqt", grad_mixed, value_rows, preferred_element_type=jnp.float32
        )
        grad_values = grad_values.at[:key_end].add(
            jnp.einsum(
                "kgqt,qkgd->tkd",
                attention.astype(jnp.bfloat16),
                grad_mixed,
                preferred_element_type=jnp.float32,
            )
        )
        row_inner = jnp.sum(attention * grad_probs, axis=-1, keepdims=True)
        grad_scores = (attention * (grad_probs - row_inner)).astype(jnp.bfloat16)
        grad_query_blocks.append(
            jnp.einsum("kgqt,tkd->qkgd", grad_scores, key_rows, preferred_element_type=jnp.float32)
            * score_scale
        )
        grad_keys = grad_keys.at[:key_end].add(
            jnp.einsum("kgqt,qkgd->tkd", grad_scores, queries, preferred_element_type=jnp.float32)
            * score_scale
        )
    grad_queries = grad_query_blocks[0].reshape(row_count, HEADS, HEAD_DIM)
    grad_queries = (
        rotate_back(grad_queries, cosine_table, sine_table)
        .reshape(row_count, D)
        .astype(jnp.bfloat16)
    )
    grad_keys = (
        rotate_back(grad_keys, cosine_table, sine_table)
        .reshape(row_count, width_kv)
        .astype(jnp.bfloat16)
    )
    grad_values = grad_values.reshape(row_count, width_kv).astype(jnp.bfloat16)
    grad_wquery = left_dot(normed_one, grad_queries)
    grad_wkey = left_dot(normed_one, grad_keys)
    grad_wvalue = left_dot(normed_one, grad_values)
    grad_normed_one = (
        right_dot(grad_queries, mat_query)
        + right_dot(grad_keys, mat_key)
        + right_dot(grad_values, mat_value)
    )
    grad_input_norm, gain_one = norm_backward(grad_normed_one, unit_one, inverse_one, norm_gains[0])
    input_grad = (grad_residual + grad_input_norm).astype(jnp.bfloat16)
    gain_one, gain_two = lax.psum((gain_one, gain_two), "fsdp")
    gain_grads = jnp.stack([gain_one, gain_two])
    shards = (
        lax.psum_scatter(grad_wquery.reshape(-1), "fsdp", scatter_dimension=0, tiled=True),
        lax.psum_scatter(grad_wkey.reshape(-1), "fsdp", scatter_dimension=0, tiled=True),
        lax.psum_scatter(grad_wvalue.reshape(-1), "fsdp", scatter_dimension=0, tiled=True),
        lax.psum_scatter(grad_woutput.reshape(-1), "fsdp", scatter_dimension=0, tiled=True),
        lax.psum_scatter(grad_wgate.reshape(-1), "fsdp", scatter_dimension=0, tiled=True),
        lax.psum_scatter(grad_wup.reshape(-1), "fsdp", scatter_dimension=0, tiled=True),
        lax.psum_scatter(grad_wdown.reshape(-1), "fsdp", scatter_dimension=0, tiled=True),
    )
    return (
        output,
        input_grad,
        gain_grads,
        shards[0],
        shards[1],
        shards[2],
        shards[3],
        shards[4],
        shards[5],
        shards[6],
    )


RANKS = 32
LAYERS = 4
ROWS = 16
WIDE = 4096
TALL = 80
LANES = 640
MESH = pl.DeviceIdType.MESH


def place():
    me = lax.axis_index("fsdp")
    return me, me // 8, me % 8, me % 2


def near_order(z):
    half = z // 2
    return (z, 1 - z + 4 * half, 2 - half, 3 - 3 * half)


def flip(index, bit):
    return index + bit - 2 * bit * ((index // bit) % 2)


def meet(me, z, bits):
    barrier = pltpu.get_barrier_semaphore()
    for bit in bits:
        pl.semaphore_signal(barrier, inc=1, device_id=(flip(me, bit),), device_id_type=MESH)

    @pl.when(z > 0)
    def _():
        pl.semaphore_signal(barrier, inc=1, device_id=(me - 8,), device_id_type=MESH)

    @pl.when(z < LAYERS - 1)
    def _():
        pl.semaphore_signal(barrier, inc=1, device_id=(me + 8,), device_id_type=MESH)

    pl.semaphore_wait(barrier, len(bits) + 1 + ((z + 1) // 2) % 2)


def gather_kernel(wide_in, tall_in, wide_out, tall_out, own_sem, send_sem, recv_sem):
    me, z, rest, core = place()
    outs = (wide_out, tall_out)
    ins = (wide_in, tall_in)

    def copy(kind, part, slot, target, own=False):
        return pltpu.make_async_remote_copy(
            src_ref=ins[part] if own else outs[part].at[slot],
            dst_ref=outs[part].at[slot],
            send_sem=send_sem.at[kind, part, slot],
            recv_sem=recv_sem.at[part, slot],
            device_id=(target,),
            device_id_type=MESH,
        )

    sends = []

    def send(kind, part, slot, target, own=False, when=None):
        sends.append((kind, part, slot, target, own, when))
        if when is None:
            copy(kind, part, slot, target, own).start()
        else:

            @pl.when(when)
            def _():
                copy(kind, part, slot, target, own).start()

    def arrive(part, slot):
        copy(0, part, slot, me).wait_recv()

    def along(slot, layer, own):
        for part in (0, 1):
            if own:
                send(0, part, slot, me + 8, own, z < LAYERS - 1)
                send(1, part, slot, me - 8, own, z > 0)
            else:
                send(0, part, slot, me + 8, own, (layer < z) & (z < LAYERS - 1))
                send(1, part, slot, me - 8, own, (layer > z) & (z > 0))

    def around(slot, own):
        send(2, 0, slot, flip(me, 2), own)
        send(3, 1, slot, flip(me, 4), own)
        send(2, 1, slot, flip(me, 2), own)
        send(3, 0, slot, flip(me, 4), own)

    meet(me, z, (1, 2, 4))
    order = near_order(z)
    along(me, z, True)
    around(me, True)
    for part in (0, 1):
        send(4, part, me, flip(me, 1), True)
        pltpu.make_async_copy(ins[part], outs[part].at[me], own_sem.at[part]).start()

    def same(layer):
        slot = layer * 8 + rest
        for part in (0, 1):
            arrive(part, slot)
        along(slot, layer, False)
        around(slot, False)
        for part in (0, 1):
            send(4, part, slot, flip(me, 1))

    def beside(layer):
        slot = layer * 8 + rest
        by_x, by_y = flip(slot, 2), flip(slot, 4)
        arrive(0, by_x)
        send(3, 0, by_x, flip(me, 4))
        arrive(1, by_y)
        send(2, 1, by_y, flip(me, 2))
        arrive(1, by_x)
        arrive(0, by_y)
        for part, at in ((0, by_x), (1, by_y), (1, by_x), (0, by_y)):
            send(4, part, at, flip(me, 1))

    def across(layer):
        slot = flip(flip(layer * 8 + rest, 2), 4)
        for part in (0, 1):
            arrive(part, slot)
            send(4, part, slot, flip(me, 1))

    for step in range(1, LAYERS):
        same(order[step])
        beside(order[step - 1])
    beside(order[LAYERS - 1])
    for step in range(LAYERS):
        across(order[step])
    for layer in range(LAYERS):
        for pair in range(4):
            for part in (0, 1):
                arrive(part, layer * 8 + pair * 2 + 1 - core)
    for part in (0, 1):
        pltpu.make_async_copy(ins[part], outs[part].at[me], own_sem.at[part]).wait()
    for kind, part, slot, target, own, when in sends:
        if when is None:
            copy(kind, part, slot, target, own).wait_send()
        else:

            @pl.when(when)
            def _(kind=kind, part=part, slot=slot, target=target, own=own):
                copy(kind, part, slot, target, own).wait_send()


def gather_slabs(wide, tall):
    return pl.pallas_call(
        gather_kernel,
        out_shape=(
            jax.ShapeDtypeStruct((RANKS, ROWS, WIDE), jnp.bfloat16),
            jax.ShapeDtypeStruct((RANKS, TALL, LANES), jnp.bfloat16),
        ),
        in_specs=[pl.BlockSpec(memory_space=pl.ANY)] * 2,
        out_specs=[pl.BlockSpec(memory_space=pl.ANY)] * 2,
        scratch_shapes=[
            pltpu.SemaphoreType.DMA((2,)),
            pltpu.SemaphoreType.DMA((5, 2, RANKS)),
            pltpu.SemaphoreType.DMA((2, RANKS)),
        ],
        compiler_params=pltpu.CompilerParams(collective_id=0, has_side_effects=True),
        name="gather_weights",
    )(wide, tall)


def scatter_kernel(
    wide_in, tall_in, gains_in, wide_out, tall_out, gains_out,
    wide_own, tall_own, wide_sib, tall_sib, wide_hop, tall_hop, wide_diag, tall_diag,
    wide_z, tall_z, gain_mine, gain_got,
    own_sem, sib_send, sib_recv, hop_send, hop_recv, diag_send, diag_recv, z_send, z_recv,
    gain_send, gain_recv,
):
    me, z, rest, core = place()
    ins, outs = (wide_in, tall_in), (wide_out, tall_out)
    owns, sibs = (wide_own, tall_own), (wide_sib, tall_sib)
    hops, diags, zs = (wide_hop, tall_hop), (wide_diag, tall_diag), (wide_z, tall_z)
    order = near_order(z)[::-1]
    meet(me, z, (1, 2, 4, 16))

    def dest(layer, turn):
        slot = layer * 8 + rest
        if turn % 2:
            slot = flip(slot, 2)
        if turn // 2:
            slot = flip(slot, 4)
        return slot

    def own_copy(part, layer, turn):
        return pltpu.make_async_copy(
            ins[part].at[dest(layer, turn)], owns[part].at[turn, layer], own_sem.at[part, turn, layer]
        )

    def remote(src, dst, send_sem, recv_sem, target):
        return pltpu.make_async_remote_copy(
            src_ref=src, dst_ref=dst, send_sem=send_sem, recv_sem=recv_sem,
            device_id=(target,), device_id_type=MESH,
        )

    def sib_copy(part, layer, turn):
        return remote(
            ins[part].at[flip(dest(layer, turn), 1)], sibs[part].at[turn, layer],
            sib_send.at[part, turn, layer], sib_recv.at[part, turn, layer], flip(me, 1),
        )

    def diag_copy(part, layer):
        return remote(
            owns[part].at[3, layer], diags[part].at[layer],
            diag_send.at[part, layer], diag_recv.at[part, layer], flip(me, 2 if part == 0 else 4),
        )

    def hop_copy(part, layer, turn):
        return remote(
            owns[part].at[turn, layer], hops[part].at[turn - 1, layer],
            hop_send.at[part, turn - 1, layer], hop_recv.at[part, turn - 1, layer],
            flip(me, 2 if turn == 1 else 4),
        )

    def z_copy(part, layer, way):
        return remote(
            owns[part].at[0, layer], zs[part].at[way, layer],
            z_send.at[part, way, layer], z_recv.at[part, way, layer], me + 8 if way == 0 else me - 8,
        )

    def base(part, layer, turn):
        own_copy(part, layer, turn).wait()
        sib_copy(part, layer, turn).wait_recv()
        return owns[part][turn, layer].astype(jnp.float32) + sibs[part][turn, layer].astype(jnp.float32)

    def gain_copy(stage):
        return remote(
            gain_mine.at[stage], gain_got.at[stage], gain_send.at[stage], gain_recv.at[stage],
            flip(me, 2**stage),
        )

    def gain_step(stage):
        gain_copy(stage - 1).wait_recv()
        gain_mine[stage] = gain_mine[stage - 1] + gain_got[stage - 1]
        if stage < 5:
            gain_copy(stage).start()

    for turn in (3, 1, 2, 0):
        for layer in order:
            for part in (0, 1):
                sib_copy(part, layer, turn).start()
                own_copy(part, layer, turn).start()
    gain_mine[0] = gains_in[...]
    gain_copy(0).start()
    for layer in order:
        for part in (0, 1):
            owns[part][3, layer] = base(part, layer, 3).astype(jnp.bfloat16)
            diag_copy(part, layer).start()
    gain_step(1)
    for layer in order:
        for turn, part, more in ((1, 0, False), (2, 1, False), (1, 1, True), (2, 0, True)):
            total = base(part, layer, turn)
            if more:
                diag_copy(part, layer).wait_recv()
                total = total + diags[part][layer].astype(jnp.float32)
            owns[part][turn, layer] = total.astype(jnp.bfloat16)
            hop_copy(part, layer, turn).start()
        if layer is order[1]:
            gain_step(2)
    gain_step(3)

    def below(part, layer):
        z_copy(part, layer, 0).wait_recv()
        owns[part][0, layer] = (
            owns[part][0, layer].astype(jnp.float32) + zs[part][0, layer].astype(jnp.float32)
        ).astype(jnp.bfloat16)

    def above(part, layer):
        z_copy(part, layer, 1).wait_recv()
        owns[part][0, layer] = (
            owns[part][0, layer].astype(jnp.float32) + zs[part][1, layer].astype(jnp.float32)
        ).astype(jnp.bfloat16)

    for layer in order[:-1]:
        for part in (0, 1):
            total = base(part, layer, 0)
            for turn in (1, 2):
                hop_copy(part, layer, turn).wait_recv()
                total = total + hops[part][turn - 1, layer].astype(jnp.float32)
            owns[part][0, layer] = total.astype(jnp.bfloat16)
            pl.when((layer > z) & (z > 0))(functools.partial(below, part, layer))
            pl.when((layer < z) & (z < LAYERS - 1))(functools.partial(above, part, layer))
            pl.when(layer > z)(lambda: z_copy(part, layer, 0).start())
            pl.when(layer < z)(lambda: z_copy(part, layer, 1).start())
    gain_step(4)
    for part in (0, 1):
        total = base(part, z, 0)
        for turn in (1, 2):
            hop_copy(part, z, turn).wait_recv()
            total = total + hops[part][turn - 1, z].astype(jnp.float32)
        outs[part][...] = total

        @pl.when(z > 0)
        def _():
            z_copy(part, z, 0).wait_recv()
            outs[part][...] = outs[part][...] + zs[part][0, z].astype(jnp.float32)

        @pl.when(z < LAYERS - 1)
        def _():
            z_copy(part, z, 1).wait_recv()
            outs[part][...] = outs[part][...] + zs[part][1, z].astype(jnp.float32)

    gain_step(5)
    gains_out[...] = gain_mine[5]
    for stage in range(5):
        gain_copy(stage).wait_send()
    for part in (0, 1):
        for layer in order:
            for turn in range(4):
                sib_copy(part, layer, turn).wait_send()
            diag_copy(part, layer).wait_send()
            for turn in (1, 2):
                hop_copy(part, layer, turn).wait_send()
        for layer in order[:-1]:
            pl.when(layer > z)(lambda: z_copy(part, layer, 0).wait_send())
            pl.when(layer < z)(lambda: z_copy(part, layer, 1).wait_send())


def scatter_slabs(wide, tall, gains):
    shapes = ((ROWS, WIDE), (TALL, LANES))

    def buffers(*lead):
        return [pltpu.VMEM((*lead, *shape), jnp.bfloat16) for shape in shapes]

    def semaphores(*lead):
        return [pltpu.SemaphoreType.DMA((2, *lead))] * 2

    return pl.pallas_call(
        scatter_kernel,
        out_shape=(
            jax.ShapeDtypeStruct(shapes[0], jnp.float32),
            jax.ShapeDtypeStruct(shapes[1], jnp.float32),
            jax.ShapeDtypeStruct(gains.shape, jnp.float32),
        ),
        in_specs=[pl.BlockSpec(memory_space=pl.ANY)] * 2 + [pl.BlockSpec(memory_space=pltpu.VMEM)],
        out_specs=[pl.BlockSpec(memory_space=pltpu.VMEM)] * 3,
        scratch_shapes=[
            *buffers(4, LAYERS),
            *buffers(4, LAYERS),
            *buffers(2, LAYERS),
            *buffers(LAYERS),
            *buffers(2, LAYERS),
            pltpu.VMEM((6, *gains.shape), jnp.float32),
            pltpu.VMEM((5, *gains.shape), jnp.float32),
            pltpu.SemaphoreType.DMA((2, 4, LAYERS)),
            *semaphores(4, LAYERS),
            *semaphores(2, LAYERS),
            *semaphores(LAYERS),
            *semaphores(2, LAYERS),
            *[pltpu.SemaphoreType.DMA((5,))] * 2,
        ],
        compiler_params=pltpu.CompilerParams(
            collective_id=1, has_side_effects=True, vmem_limit_bytes=40 << 20
        ),
        name="scatter_gradients",
    )(wide, tall, gains)


def spread_matrix():
    rows = D // RANKS
    k = jnp.arange(D)
    main = k // ROWS * rows + k % ROWS
    late = k - RANKS * ROWS
    rest = late // (rows - ROWS) * rows + ROWS + late % (rows - ROWS)
    perm = jnp.where(k < RANKS * ROWS, main, rest)
    return (jnp.arange(D)[:, None] == perm[None, :]).astype(jnp.bfloat16)


def fast_body(
    tokens, segments, cotangent, norm_gains, w_query, w_key, w_value, w_output, w_gate, w_up, w_down
):
    row_count = tokens.shape[0]
    width_kv = KV_HEADS * HEAD_DIM
    group_size = HEADS // KV_HEADS
    score_scale = HEAD_DIM ** (-0.5)
    own_rows = D // RANKS
    down_rows = FF // RANKS
    late_rows = own_rows - ROWS
    main = RANKS * ROWS
    edges = (2 * FF, 2 * FF + D + 2 * width_kv)

    own = jnp.concatenate(
        [w.reshape(own_rows, -1) for w in (w_gate, w_up, w_query, w_key, w_value, w_output)], axis=1
    )
    wide = jnp.pad(own[:ROWS, : edges[1]], ((0, 0), (0, WIDE - edges[1])))
    tall = jnp.concatenate(
        [w_down.reshape(down_rows, D), own[:ROWS, edges[1] :], own[ROWS:].reshape(-1, D)], axis=0
    )
    tall = jnp.pad(tall, ((0, 0), (0, LANES - D)))
    wide_all, tall_all = gather_slabs(wide, tall)
    wide_all = wide_all.reshape(main, WIDE)
    mat_down = tall_all[:, :down_rows, :D].reshape(FF, D)
    late_all = tall_all[:, down_rows + ROWS :, :D].reshape(D - main, edges[1] + D)
    mat_all = jnp.concatenate([wide_all[:, : edges[1]], late_all[:, : edges[1]]], axis=0)
    mat_mlp, mat_qkv = mat_all[:, : edges[0]], mat_all[:, edges[0] :]
    mat_output = jnp.concatenate(
        [
            tall_all[:, down_rows : down_rows + ROWS, :D].reshape(main, D),
            late_all[:, edges[1] :],
        ],
        axis=0,
    )
    spread = spread_matrix()

    def spread_rows(v):
        return jnp.dot(v, spread, preferred_element_type=jnp.float32).astype(jnp.bfloat16)

    def gather_back(v):
        return lax.dot_general(
            v,
            spread.astype(jnp.float32),
            (((1,), (1,)), ((), ())),
            precision=lax.Precision.HIGHEST,
            preferred_element_type=jnp.float32,
        )

    segment_row = segments[0]
    cosine_table, sine_table = rotary_tables(segment_row)
    inputs = tokens.astype(jnp.float32)
    normed_one, unit_one, inverse_one = norm_forward(inputs, norm_gains[0])
    normed_one = spread_rows(normed_one.astype(jnp.bfloat16))
    qkv = jnp.dot(normed_one, mat_qkv, preferred_element_type=jnp.float32)
    queries = qkv[:, :D].reshape(row_count, HEADS, HEAD_DIM)
    key_rows = qkv[:, D : D + width_kv].reshape(row_count, KV_HEADS, HEAD_DIM)
    value_rows = qkv[:, D + width_kv :].astype(jnp.bfloat16).reshape(row_count, KV_HEADS, HEAD_DIM)
    queries = rotate_pairs(queries, cosine_table, sine_table).astype(jnp.bfloat16)
    queries = queries.reshape(row_count, KV_HEADS, group_size, HEAD_DIM)
    key_rows = rotate_pairs(key_rows, cosine_table, sine_table).astype(jnp.bfloat16)
    pos = jnp.arange(row_count)
    allowed = (pos[None, :] <= pos[:, None]) & (segment_row[:, None] == segment_row[None, :])
    scores = (
        jnp.einsum("qkgd,tkd->kgqt", queries, key_rows, preferred_element_type=jnp.float32)
        * score_scale
    )
    scores = jnp.where(allowed[None, None], scores, NEGATIVE)
    exp_scores = jnp.exp(scores - jnp.max(scores, axis=-1, keepdims=True))
    probs = exp_scores / jnp.sum(exp_scores, axis=-1, keepdims=True)
    attention = probs.astype(jnp.bfloat16)
    mixed = jnp.einsum("kgqt,tkd->qkgd", attention, value_rows, preferred_element_type=jnp.float32)
    mixed = spread_rows(mixed.reshape(row_count, D).astype(jnp.bfloat16))
    residual = inputs + jnp.dot(mixed, mat_output, preferred_element_type=jnp.float32)
    normed_two, unit_two, inverse_two = norm_forward(residual, norm_gains[1])
    normed_two = spread_rows(normed_two.astype(jnp.bfloat16))
    both = jnp.dot(normed_two, mat_mlp, preferred_element_type=jnp.float32)
    gate_pre, up_pre = both[:, :FF], both[:, FF:]
    sigmoid_gate = jax.nn.sigmoid(gate_pre)
    activated = gate_pre * sigmoid_gate
    hidden = (activated * up_pre).astype(jnp.bfloat16)
    output = (residual + jnp.dot(hidden, mat_down, preferred_element_type=jnp.float32)).astype(
        jnp.bfloat16
    )

    grad_wdown = left_dot(hidden, cotangent).astype(jnp.bfloat16)
    grad_hidden = right_dot(cotangent, mat_down)
    grad_gate = (
        grad_hidden * up_pre * sigmoid_gate * (1.0 + gate_pre * (1.0 - sigmoid_gate))
    ).astype(jnp.bfloat16)
    grad_up = (grad_hidden * activated).astype(jnp.bfloat16)
    grad_both = jnp.concatenate([grad_gate, grad_up], axis=1)
    grad_wboth = left_dot(normed_two, grad_both).astype(jnp.bfloat16)
    grad_normed_two = gather_back(right_dot(grad_both, mat_mlp))
    grad_from_norm, gain_two = norm_backward(grad_normed_two, unit_two, inverse_two, norm_gains[1])
    grad_residual = cotangent.astype(jnp.float32) + grad_from_norm
    grad_attn = grad_residual.astype(jnp.bfloat16)
    grad_woutput = left_dot(mixed, grad_attn).astype(jnp.bfloat16)
    grad_mixed = right_dot(grad_attn, mat_output).astype(jnp.bfloat16)
    grad_mixed = right_dot(grad_mixed, spread).astype(jnp.bfloat16)
    grad_mixed = grad_mixed.reshape(row_count, KV_HEADS, group_size, HEAD_DIM)
    grad_probs = jnp.einsum(
        "qkgd,tkd->kgqt", grad_mixed, value_rows, preferred_element_type=jnp.float32
    )
    grad_values = jnp.einsum(
        "kgqt,qkgd->tkd", attention, grad_mixed, preferred_element_type=jnp.float32
    )
    row_inner = jnp.sum(probs * grad_probs, axis=-1, keepdims=True)
    grad_scores = (probs * (grad_probs - row_inner)).astype(jnp.bfloat16)
    grad_queries = (
        jnp.einsum("kgqt,tkd->qkgd", grad_scores, key_rows, preferred_element_type=jnp.float32)
        * score_scale
    ).reshape(row_count, HEADS, HEAD_DIM)
    grad_keys = (
        jnp.einsum("kgqt,qkgd->tkd", grad_scores, queries, preferred_element_type=jnp.float32)
        * score_scale
    )
    grad_queries = rotate_back(grad_queries, cosine_table, sine_table).reshape(row_count, D)
    grad_keys = rotate_back(grad_keys, cosine_table, sine_table).reshape(row_count, width_kv)
    grad_qkv = jnp.concatenate(
        [grad_queries, grad_keys, grad_values.reshape(row_count, width_kv)], axis=1
    ).astype(jnp.bfloat16)
    grad_wqkv = left_dot(normed_one, grad_qkv).astype(jnp.bfloat16)
    grad_normed_one = gather_back(right_dot(grad_qkv, mat_qkv))
    grad_input_norm, gain_one = norm_backward(grad_normed_one, unit_one, inverse_one, norm_gains[0])
    input_grad = (grad_residual + grad_input_norm).astype(jnp.bfloat16)

    grad_wide = jnp.concatenate(
        [grad_wboth[:main], grad_wqkv[:main], jnp.zeros((main, WIDE - edges[1]), jnp.bfloat16)],
        axis=1,
    ).reshape(RANKS, ROWS, WIDE)
    grad_late = jnp.concatenate([grad_wboth[main:], grad_wqkv[main:], grad_woutput[main:]], axis=1)
    grad_tall = jnp.concatenate(
        [
            grad_wdown.reshape(RANKS, down_rows, D),
            grad_woutput[:main].reshape(RANKS, ROWS, D),
            grad_late.reshape(RANKS, ROWS, D),
        ],
        axis=1,
    )
    grad_tall = jnp.pad(grad_tall, ((0, 0), (0, 0), (0, LANES - D)))
    gains = jnp.pad(jnp.stack([gain_one, gain_two]), ((0, 6), (0, LANES - D)))
    sum_wide, sum_tall, sum_gains = scatter_slabs(grad_wide, grad_tall, gains)
    late = sum_tall[down_rows + ROWS :, :D].reshape(late_rows, edges[1] + D)
    own_sum = jnp.concatenate([sum_wide[:, : edges[1]], late[:, : edges[1]]], axis=0)
    own_output = jnp.concatenate([sum_tall[down_rows : down_rows + ROWS, :D], late[:, edges[1] :]])
    cuts = (0, FF, 2 * FF, 2 * FF + D, 2 * FF + D + width_kv, 2 * FF + D + 2 * width_kv)
    gate, up, query, key, value = (
        own_sum[:, low:high].reshape(-1) for low, high in zip(cuts[:-1], cuts[1:])
    )
    return (
        output,
        input_grad,
        sum_gains[:2, :D],
        query,
        key,
        value,
        own_output.reshape(-1),
        gate,
        up,
        sum_tall[:down_rows, :D].reshape(-1),
    )


def solution(mesh):
    placed = (
        P("fsdp", None),
        P("fsdp", None),
        P("fsdp", None),
        P(),
        P("fsdp"),
        P("fsdp"),
        P("fsdp"),
        P("fsdp"),
        P("fsdp"),
        P("fsdp"),
        P("fsdp"),
    )
    return jax.shard_map(
        fast_body if mesh.shape["fsdp"] == RANKS else plain_body,
        mesh=mesh,
        in_specs=placed,
        out_specs=(
            P("fsdp", None),
            P("fsdp", None),
            P(),
            P("fsdp"),
            P("fsdp"),
            P("fsdp"),
            P("fsdp"),
            P("fsdp"),
            P("fsdp"),
            P("fsdp"),
        ),
        check_vma=False,
    )
```

```python
import functools
import math

import jax
import jax.numpy as jnp
from jax import lax
from jax.experimental import pallas as pl
from jax.experimental.pallas import tpu as pltpu
from jax.sharding import PartitionSpec as P

D = 576
FF = 1536
HEADS = 9
KV_HEADS = 3
HEAD_DIM = 64
DOCS = 3


EPSILON = 1e-05
THETA = 100000.0
NEGATIVE = -1e30


def rotary_tables(segment_row):
    length = segment_row.shape[0]
    positions = jnp.arange(length, dtype=jnp.int32)
    doc_ids = jnp.arange(DOCS, dtype=jnp.int32)
    starts = jnp.sum((segment_row[None, :] < doc_ids[:, None]).astype(jnp.int32), axis=1)
    member = (segment_row[:, None] == doc_ids[None, :]).astype(jnp.int32)
    offsets = positions - jnp.sum(member * starts[None, :], axis=1)
    frequency = jnp.exp(
        jnp.arange(0, HEAD_DIM, 2).astype(jnp.float32) * (-math.log(THETA) / HEAD_DIM)
    )
    angles = offsets.astype(jnp.float32)[:, None] * frequency[None, :]
    angles = jnp.concatenate([angles, angles], axis=1)
    return (jnp.cos(angles), jnp.sin(angles))


def rotate_pairs(vectors, cosine_table, sine_table):
    half_width = vectors.shape[-1] // 2
    turned = jnp.concatenate([-vectors[..., half_width:], vectors[..., :half_width]], axis=-1)
    return vectors * cosine_table[:, None, :] + turned * sine_table[:, None, :]


def rotate_back(gradient, cosine_table, sine_table):
    half_width = gradient.shape[-1] // 2
    scaled = gradient * sine_table[:, None, :]
    turned = jnp.concatenate([scaled[..., half_width:], -scaled[..., :half_width]], axis=-1)
    return gradient * cosine_table[:, None, :] + turned


def norm_forward(vectors, gain_row):
    inverse = lax.rsqrt(jnp.mean(vectors * vectors, axis=-1, keepdims=True) + EPSILON)
    unit_rows = vectors * inverse
    return (unit_rows * gain_row, unit_rows, inverse)


def norm_backward(upstream, unit_rows, inverse, gain_row):
    scaled = upstream * gain_row
    grad_in = inverse * (scaled - unit_rows * jnp.mean(scaled * unit_rows, axis=-1, keepdims=True))
    return (grad_in, jnp.sum(upstream * unit_rows, axis=0))


def left_dot(first, second):
    return lax.dot_general(
        first, second, (((0,), (0,)), ((), ())), preferred_element_type=jnp.float32
    )


def right_dot(first, second):
    return lax.dot_general(
        first, second, (((1,), (1,)), ((), ())), preferred_element_type=jnp.float32
    )


def attn_shapes(flat_list):
    width_kv = KV_HEADS * HEAD_DIM
    return (
        flat_list[0].reshape(D, D),
        flat_list[1].reshape(D, width_kv),
        flat_list[2].reshape(D, width_kv),
        flat_list[3].reshape(D, D),
    )


def mlp_shapes(flat_list):
    return (flat_list[0].reshape(D, FF), flat_list[1].reshape(D, FF), flat_list[2].reshape(FF, D))


def plain_body(
    tokens, segments, cotangent, norm_gains, w_query, w_key, w_value, w_output, w_gate, w_up, w_down
):
    row_count = tokens.shape[0]
    width_kv = KV_HEADS * HEAD_DIM
    group_size = HEADS // KV_HEADS
    score_scale = HEAD_DIM ** (-0.5)
    block_rows = min(512, row_count)
    segment_row = segments[0]
    cosine_table, sine_table = rotary_tables(segment_row)
    inputs = tokens.astype(jnp.float32)
    attn_flat = (
        lax.all_gather(w_query, "fsdp", axis=0, tiled=True),
        lax.all_gather(w_key, "fsdp", axis=0, tiled=True),
        lax.all_gather(w_value, "fsdp", axis=0, tiled=True),
        lax.all_gather(w_output, "fsdp", axis=0, tiled=True),
    )
    mat_query, mat_key, mat_value, mat_output = attn_shapes(attn_flat)
    normed_one, unit_one, inverse_one = norm_forward(inputs, norm_gains[0])
    normed_one = normed_one.astype(jnp.bfloat16)
    queries = jnp.dot(normed_one, mat_query, preferred_element_type=jnp.float32).reshape(
        row_count, HEADS, HEAD_DIM
    )
    key_rows = jnp.dot(normed_one, mat_key, preferred_element_type=jnp.float32).reshape(
        row_count, KV_HEADS, HEAD_DIM
    )
    value_rows = jnp.dot(normed_one, mat_value, preferred_element_type=jnp.float32).astype(
        jnp.bfloat16
    )
    value_rows = value_rows.reshape(row_count, KV_HEADS, HEAD_DIM)
    queries = rotate_pairs(queries, cosine_table, sine_table).astype(jnp.bfloat16)
    queries = queries.reshape(row_count, KV_HEADS, group_size, HEAD_DIM)
    key_rows = rotate_pairs(key_rows, cosine_table, sine_table).astype(jnp.bfloat16)

    def block_scores(block_start, key_end):
        query_pos = block_start + jnp.arange(block_rows)
        key_pos = jnp.arange(key_end)
        causal = key_pos[None, :] <= query_pos[:, None]
        same_doc = segment_row[:, None] == segment_row[None, :]
        scores = (
            jnp.einsum("qkgd,tkd->kgqt", queries, key_rows, preferred_element_type=jnp.float32)
            * score_scale
        )
        return jnp.where((causal & same_doc)[None, None], scores, NEGATIVE)

    block_start = 0
    key_end = block_start + block_rows
    scores = block_scores(block_start, key_end)
    row_peak = jnp.max(scores, axis=-1, keepdims=True)
    exp_scores = jnp.exp(scores - row_peak)
    row_total = jnp.sum(exp_scores, axis=-1, keepdims=True)
    attention = (exp_scores / row_total).astype(jnp.bfloat16)
    logsum_blocks = [row_peak + jnp.log(row_total)]
    mixed_blocks = jnp.einsum(
        "kgqt,tkd->qkgd", attention, value_rows, preferred_element_type=jnp.float32
    )
    mixed = mixed_blocks.reshape(row_count, D).astype(jnp.bfloat16)
    residual = inputs + jnp.dot(mixed, mat_output, preferred_element_type=jnp.float32)
    mlp_flat = (
        lax.all_gather(w_gate, "fsdp", axis=0, tiled=True),
        lax.all_gather(w_up, "fsdp", axis=0, tiled=True),
        lax.all_gather(w_down, "fsdp", axis=0, tiled=True),
    )
    mat_gate, mat_up, mat_down = mlp_shapes(mlp_flat)
    normed_two, unit_two, inverse_two = norm_forward(residual, norm_gains[1])
    normed_two = normed_two.astype(jnp.bfloat16)
    gate_pre = jnp.dot(normed_two, mat_gate, preferred_element_type=jnp.float32)
    up_pre = jnp.dot(normed_two, mat_up, preferred_element_type=jnp.float32)
    activated = jax.nn.silu(gate_pre)
    hidden = (activated * up_pre).astype(jnp.bfloat16)
    output = (residual + jnp.dot(hidden, mat_down, preferred_element_type=jnp.float32)).astype(
        jnp.bfloat16
    )
    mlp_flat = (
        lax.all_gather(w_gate, "fsdp", axis=0, tiled=True),
        lax.all_gather(w_up, "fsdp", axis=0, tiled=True),
        lax.all_gather(w_down, "fsdp", axis=0, tiled=True),
    )
    mat_gate, mat_up, mat_down = mlp_shapes(mlp_flat)
    grad_wdown = left_dot(hidden, cotangent)
    grad_hidden = right_dot(cotangent, mat_down)
    sigmoid_gate = jax.nn.sigmoid(gate_pre)
    grad_gate = (
        grad_hidden * up_pre * sigmoid_gate * (1.0 + gate_pre * (1.0 - sigmoid_gate))
    ).astype(jnp.bfloat16)
    grad_up = (grad_hidden * activated).astype(jnp.bfloat16)
    grad_wgate = left_dot(normed_two, grad_gate)
    grad_wup = left_dot(normed_two, grad_up)
    grad_normed_two = right_dot(grad_gate, mat_gate) + right_dot(grad_up, mat_up)
    grad_from_norm, gain_two = norm_backward(grad_normed_two, unit_two, inverse_two, norm_gains[1])
    grad_residual = cotangent.astype(jnp.float32) + grad_from_norm
    attn_flat = (
        lax.all_gather(w_query, "fsdp", axis=0, tiled=True),
        lax.all_gather(w_key, "fsdp", axis=0, tiled=True),
        lax.all_gather(w_value, "fsdp", axis=0, tiled=True),
        lax.all_gather(w_output, "fsdp", axis=0, tiled=True),
    )
    mat_query, mat_key, mat_value, mat_output = attn_shapes(attn_flat)
    grad_attn = grad_residual.astype(jnp.bfloat16)
    grad_woutput = left_dot(mixed, grad_attn)
    grad_mixed = right_dot(grad_attn, mat_output).astype(jnp.bfloat16)
    grad_mixed = grad_mixed.reshape(row_count, KV_HEADS, group_size, HEAD_DIM)
    grad_query_blocks = []
    grad_keys = jnp.zeros((row_count, KV_HEADS, HEAD_DIM), jnp.float32)
    grad_values = jnp.zeros((row_count, KV_HEADS, HEAD_DIM), jnp.float32)
    for block_index, block_start in enumerate(range(0, row_count, block_rows)):
        key_end = block_start + block_rows
        scores = block_scores(block_start, key_end)
        attention = jnp.exp(scores - logsum_blocks[block_index])
        grad_probs = jnp.einsum(
            "qkgd,tkd->kgqt", grad_mixed, value_rows, preferred_element_type=jnp.float32
        )
        grad_values = grad_values.at[:key_end].add(
            jnp.einsum(
                "kgqt,qkgd->tkd",
                attention.astype(jnp.bfloat16),
                grad_mixed,
                preferred_element_type=jnp.float32,
            )
        )
        row_inner = jnp.sum(attention * grad_probs, axis=-1, keepdims=True)
        grad_scores = (attention * (grad_probs - row_inner)).astype(jnp.bfloat16)
        grad_query_blocks.append(
            jnp.einsum("kgqt,tkd->qkgd", grad_scores, key_rows, preferred_element_type=jnp.float32)
            * score_scale
        )
        grad_keys = grad_keys.at[:key_end].add(
            jnp.einsum("kgqt,qkgd->tkd", grad_scores, queries, preferred_element_type=jnp.float32)
            * score_scale
        )
    grad_queries = grad_query_blocks[0].reshape(row_count, HEADS, HEAD_DIM)
    grad_queries = (
        rotate_back(grad_queries, cosine_table, sine_table)
        .reshape(row_count, D)
        .astype(jnp.bfloat16)
    )
    grad_keys = (
        rotate_back(grad_keys, cosine_table, sine_table)
        .reshape(row_count, width_kv)
        .astype(jnp.bfloat16)
    )
    grad_values = grad_values.reshape(row_count, width_kv).astype(jnp.bfloat16)
    grad_wquery = left_dot(normed_one, grad_queries)
    grad_wkey = left_dot(normed_one, grad_keys)
    grad_wvalue = left_dot(normed_one, grad_values)
    grad_normed_one = (
        right_dot(grad_queries, mat_query)
        + right_dot(grad_keys, mat_key)
        + right_dot(grad_values, mat_value)
    )
    grad_input_norm, gain_one = norm_backward(grad_normed_one, unit_one, inverse_one, norm_gains[0])
    input_grad = (grad_residual + grad_input_norm).astype(jnp.bfloat16)
    gain_one, gain_two = lax.psum((gain_one, gain_two), "fsdp")
    gain_grads = jnp.stack([gain_one, gain_two])
    shards = (
        lax.psum_scatter(grad_wquery.reshape(-1), "fsdp", scatter_dimension=0, tiled=True),
        lax.psum_scatter(grad_wkey.reshape(-1), "fsdp", scatter_dimension=0, tiled=True),
        lax.psum_scatter(grad_wvalue.reshape(-1), "fsdp", scatter_dimension=0, tiled=True),
        lax.psum_scatter(grad_woutput.reshape(-1), "fsdp", scatter_dimension=0, tiled=True),
        lax.psum_scatter(grad_wgate.reshape(-1), "fsdp", scatter_dimension=0, tiled=True),
        lax.psum_scatter(grad_wup.reshape(-1), "fsdp", scatter_dimension=0, tiled=True),
        lax.psum_scatter(grad_wdown.reshape(-1), "fsdp", scatter_dimension=0, tiled=True),
    )
    return (
        output,
        input_grad,
        gain_grads,
        shards[0],
        shards[1],
        shards[2],
        shards[3],
        shards[4],
        shards[5],
        shards[6],
    )


RANKS = 32
LAYERS = 4
ROWS = 16
LATE = 5120
LANES = 640
SHAPES = ((16, 3072), (16, 1024), (48, LANES), (16, LANES), (16, LANES))
PARTS = tuple(range(len(SHAPES)))
FIRST_X = (0, 3)
FIRST_Y = (1, 2, 4)
MESH = pl.DeviceIdType.MESH


def place():
    me = lax.axis_index("fsdp")
    return me, me // 8, me % 8, me % 2


def near_order(z):
    half = z // 2
    return (z, 1 - z + 4 * half, 2 - half, 3 - 3 * half)


def flip(index, bit):
    return index + bit - 2 * bit * ((index // bit) % 2)


def meet(me, z, bits):
    barrier = pltpu.get_barrier_semaphore()
    for bit in bits:
        pl.semaphore_signal(barrier, inc=1, device_id=(flip(me, bit),), device_id_type=MESH)

    @pl.when(z > 0)
    def _():
        pl.semaphore_signal(barrier, inc=1, device_id=(me - 8,), device_id_type=MESH)

    @pl.when(z < LAYERS - 1)
    def _():
        pl.semaphore_signal(barrier, inc=1, device_id=(me + 8,), device_id_type=MESH)

    pl.semaphore_wait(barrier, len(bits) + 1 + ((z + 1) // 2) % 2)


def gather_kernel(*refs):
    ins, outs = refs[: len(PARTS)], refs[len(PARTS) : 2 * len(PARTS)]
    own_sem, send_sem, recv_sem = refs[2 * len(PARTS) :]
    me, z, rest, core = place()

    def copy(kind, part, slot, target, own=False):
        return pltpu.make_async_remote_copy(
            src_ref=ins[part] if own else outs[part].at[slot],
            dst_ref=outs[part].at[slot],
            send_sem=send_sem.at[kind, part, slot],
            recv_sem=recv_sem.at[part, slot],
            device_id=(target,),
            device_id_type=MESH,
        )

    sends = []

    def send(kind, part, slot, target, own=False, when=None):
        sends.append((kind, part, slot, target, own, when))
        if when is None:
            copy(kind, part, slot, target, own).start()
        else:

            @pl.when(when)
            def _():
                copy(kind, part, slot, target, own).start()

    def arrive(part, slot):
        copy(0, part, slot, me).wait_recv()

    def along(slot, layer, own):
        for part in PARTS:
            if own:
                send(0, part, slot, me + 8, own, z < LAYERS - 1)
                send(1, part, slot, me - 8, own, z > 0)
            else:
                send(0, part, slot, me + 8, own, (layer < z) & (z < LAYERS - 1))
                send(1, part, slot, me - 8, own, (layer > z) & (z > 0))

    def around(slot, own):
        for part in FIRST_X + FIRST_Y:
            send(2, part, slot, flip(me, 2), own)
        for part in FIRST_Y + FIRST_X:
            send(3, part, slot, flip(me, 4), own)

    meet(me, z, (1, 2, 4))
    order = near_order(z)
    along(me, z, True)
    around(me, True)
    for part in PARTS:
        send(4, part, me, flip(me, 1), True)
        pltpu.make_async_copy(ins[part], outs[part].at[me], own_sem.at[part]).start()

    def same(layer):
        slot = layer * 8 + rest
        for part in PARTS:
            arrive(part, slot)
        along(slot, layer, False)
        around(slot, False)
        for part in PARTS:
            send(4, part, slot, flip(me, 1))

    def beside(layer):
        slot = layer * 8 + rest
        by_x, by_y = flip(slot, 2), flip(slot, 4)
        for part in FIRST_X:
            arrive(part, by_x)
            send(3, part, by_x, flip(me, 4))
        for part in FIRST_Y:
            arrive(part, by_y)
            send(2, part, by_y, flip(me, 2))
        for part in FIRST_Y:
            arrive(part, by_x)
        for part in FIRST_X:
            arrive(part, by_y)
        for part in PARTS:
            send(4, part, by_x, flip(me, 1))
            send(4, part, by_y, flip(me, 1))

    def across(layer):
        slot = flip(flip(layer * 8 + rest, 2), 4)
        for part in PARTS:
            arrive(part, slot)
            send(4, part, slot, flip(me, 1))

    for step in range(1, LAYERS):
        same(order[step])
        beside(order[step - 1])
    beside(order[LAYERS - 1])
    for step in range(LAYERS):
        across(order[step])
    for layer in range(LAYERS):
        for pair in range(4):
            for part in PARTS:
                arrive(part, layer * 8 + pair * 2 + 1 - core)
    for part in PARTS:
        pltpu.make_async_copy(ins[part], outs[part].at[me], own_sem.at[part]).wait()
    for kind, part, slot, target, own, when in sends:
        if when is None:
            copy(kind, part, slot, target, own).wait_send()
        else:

            @pl.when(when)
            def _(kind=kind, part=part, slot=slot, target=target, own=own):
                copy(kind, part, slot, target, own).wait_send()


def gather_slabs(slabs):
    count = len(PARTS)
    return pl.pallas_call(
        gather_kernel,
        out_shape=[jax.ShapeDtypeStruct((RANKS, *shape), jnp.bfloat16) for shape in SHAPES],
        in_specs=[pl.BlockSpec(memory_space=pl.ANY)] * count,
        out_specs=[pl.BlockSpec(memory_space=pl.ANY)] * count,
        scratch_shapes=[
            pltpu.SemaphoreType.DMA((count,)),
            pltpu.SemaphoreType.DMA((5, count, RANKS)),
            pltpu.SemaphoreType.DMA((count, RANKS)),
        ],
        compiler_params=pltpu.CompilerParams(collective_id=0, has_side_effects=True),
        name="gather_weights",
    )(*slabs)


def scatter_kernel(*refs):
    groups, at = [], 0
    for extra in (1, 1, 0, 0, 0, 0, 0):
        groups.append(refs[at : at + len(PARTS) + extra])
        at += len(PARTS) + extra
    ins, outs, owns, sibs, hops, diags, zs = groups
    gains_in, gains_out = ins[-1], outs[-1]
    (
        gain_mine, gain_got, own_sem, sib_send, sib_recv, hop_send, hop_recv, diag_send, diag_recv,
        z_send, z_recv, gain_send, gain_recv,
    ) = refs[at:]
    me, z, rest, core = place()
    order = near_order(z)[::-1]
    meet(me, z, (1, 2, 4, 16))

    def dest(layer, turn):
        slot = layer * 8 + rest
        if turn % 2:
            slot = flip(slot, 2)
        if turn // 2:
            slot = flip(slot, 4)
        return slot

    def own_copy(part, layer, turn):
        return pltpu.make_async_copy(
            ins[part].at[dest(layer, turn)], owns[part].at[turn, layer], own_sem.at[part, turn, layer]
        )

    def remote(src, dst, send_sem, recv_sem, target):
        return pltpu.make_async_remote_copy(
            src_ref=src, dst_ref=dst, send_sem=send_sem, recv_sem=recv_sem,
            device_id=(target,), device_id_type=MESH,
        )

    def sib_copy(part, layer, turn):
        return remote(
            ins[part].at[flip(dest(layer, turn), 1)], sibs[part].at[turn, layer],
            sib_send.at[part, turn, layer], sib_recv.at[part, turn, layer], flip(me, 1),
        )

    def diag_copy(part, layer):
        return remote(
            owns[part].at[3, layer], diags[part].at[layer],
            diag_send.at[part, layer], diag_recv.at[part, layer], flip(me, 2 if part in FIRST_X else 4),
        )

    def hop_copy(part, layer, turn):
        return remote(
            owns[part].at[turn, layer], hops[part].at[turn - 1, layer],
            hop_send.at[part, turn - 1, layer], hop_recv.at[part, turn - 1, layer],
            flip(me, 2 if turn == 1 else 4),
        )

    def z_copy(part, layer, way):
        return remote(
            owns[part].at[0, layer], zs[part].at[way, layer],
            z_send.at[part, way, layer], z_recv.at[part, way, layer], me + 8 if way == 0 else me - 8,
        )

    def base(part, layer, turn):
        own_copy(part, layer, turn).wait()
        sib_copy(part, layer, turn).wait_recv()
        return owns[part][turn, layer].astype(jnp.float32) + sibs[part][turn, layer].astype(jnp.float32)

    def gain_copy(stage):
        return remote(
            gain_mine.at[stage], gain_got.at[stage], gain_send.at[stage], gain_recv.at[stage],
            flip(me, 2**stage),
        )

    def gain_step(stage):
        gain_copy(stage - 1).wait_recv()
        gain_mine[stage] = gain_mine[stage - 1] + gain_got[stage - 1]
        if stage < 5:
            gain_copy(stage).start()

    for turn in (3, 1, 2, 0):
        for layer in order:
            for part in PARTS:
                sib_copy(part, layer, turn).start()
                own_copy(part, layer, turn).start()
    gain_mine[0] = gains_in[...]
    gain_copy(0).start()
    for layer in order:
        for part in PARTS:
            owns[part][3, layer] = base(part, layer, 3).astype(jnp.bfloat16)
            diag_copy(part, layer).start()
    gain_step(1)
    for layer in order:
        for turn, part, more in (
            *[(1, part, False) for part in FIRST_X],
            *[(2, part, False) for part in FIRST_Y],
            *[(1, part, True) for part in FIRST_Y],
            *[(2, part, True) for part in FIRST_X],
        ):
            total = base(part, layer, turn)
            if more:
                diag_copy(part, layer).wait_recv()
                total = total + diags[part][layer].astype(jnp.float32)
            owns[part][turn, layer] = total.astype(jnp.bfloat16)
            hop_copy(part, layer, turn).start()
        if layer is order[1]:
            gain_step(2)
    gain_step(3)

    def below(part, layer):
        z_copy(part, layer, 0).wait_recv()
        owns[part][0, layer] = (
            owns[part][0, layer].astype(jnp.float32) + zs[part][0, layer].astype(jnp.float32)
        ).astype(jnp.bfloat16)

    def above(part, layer):
        z_copy(part, layer, 1).wait_recv()
        owns[part][0, layer] = (
            owns[part][0, layer].astype(jnp.float32) + zs[part][1, layer].astype(jnp.float32)
        ).astype(jnp.bfloat16)

    for layer in order[:-1]:
        for part in PARTS:
            total = base(part, layer, 0)
            for turn in (1, 2):
                hop_copy(part, layer, turn).wait_recv()
                total = total + hops[part][turn - 1, layer].astype(jnp.float32)
            owns[part][0, layer] = total.astype(jnp.bfloat16)
            pl.when((layer > z) & (z > 0))(functools.partial(below, part, layer))
            pl.when((layer < z) & (z < LAYERS - 1))(functools.partial(above, part, layer))
            pl.when(layer > z)(lambda: z_copy(part, layer, 0).start())
            pl.when(layer < z)(lambda: z_copy(part, layer, 1).start())
    gain_step(4)
    for part in PARTS:
        total = base(part, z, 0)
        for turn in (1, 2):
            hop_copy(part, z, turn).wait_recv()
            total = total + hops[part][turn - 1, z].astype(jnp.float32)
        outs[part][...] = total

        @pl.when(z > 0)
        def _():
            z_copy(part, z, 0).wait_recv()
            outs[part][...] = outs[part][...] + zs[part][0, z].astype(jnp.float32)

        @pl.when(z < LAYERS - 1)
        def _():
            z_copy(part, z, 1).wait_recv()
            outs[part][...] = outs[part][...] + zs[part][1, z].astype(jnp.float32)

    gain_step(5)
    gains_out[...] = gain_mine[5]
    for stage in range(5):
        gain_copy(stage).wait_send()
    for part in PARTS:
        for layer in order:
            for turn in range(4):
                sib_copy(part, layer, turn).wait_send()
            diag_copy(part, layer).wait_send()
            for turn in (1, 2):
                hop_copy(part, layer, turn).wait_send()
        for layer in order[:-1]:
            pl.when(layer > z)(lambda: z_copy(part, layer, 0).wait_send())
            pl.when(layer < z)(lambda: z_copy(part, layer, 1).wait_send())


def scatter_slabs(slabs, gains):
    count = len(PARTS)
    vmem = pl.BlockSpec(memory_space=pltpu.VMEM)

    def buffers(*lead):
        return [pltpu.VMEM((*lead, *shape), jnp.bfloat16) for shape in SHAPES]

    def semaphores(*lead):
        return [pltpu.SemaphoreType.DMA((count, *lead))] * 2

    return pl.pallas_call(
        scatter_kernel,
        out_shape=[jax.ShapeDtypeStruct(shape, jnp.float32) for shape in (*SHAPES, gains.shape)],
        in_specs=[pl.BlockSpec(memory_space=pl.ANY)] * count + [vmem],
        out_specs=[vmem] * (count + 1),
        scratch_shapes=[
            *buffers(4, LAYERS),
            *buffers(4, LAYERS),
            *buffers(2, LAYERS),
            *buffers(LAYERS),
            *buffers(2, LAYERS),
            pltpu.VMEM((6, *gains.shape), jnp.float32),
            pltpu.VMEM((5, *gains.shape), jnp.float32),
            pltpu.SemaphoreType.DMA((count, 4, LAYERS)),
            *semaphores(4, LAYERS),
            *semaphores(2, LAYERS),
            *semaphores(LAYERS),
            *semaphores(2, LAYERS),
            *[pltpu.SemaphoreType.DMA((5,))] * 2,
        ],
        compiler_params=pltpu.CompilerParams(
            collective_id=1, has_side_effects=True, vmem_limit_bytes=40 << 20
        ),
        name="scatter_gradients",
    )(*slabs, gains)


def spread_matrix():
    rows = D // RANKS
    k = jnp.arange(D)
    main = k // ROWS * rows + k % ROWS
    late = k - RANKS * ROWS
    rest = late // (rows - ROWS) * rows + ROWS + late % (rows - ROWS)
    perm = jnp.where(k < RANKS * ROWS, main, rest)
    return (jnp.arange(D)[:, None] == perm[None, :]).astype(jnp.bfloat16)


def fast_body(
    tokens, segments, cotangent, norm_gains, w_query, w_key, w_value, w_output, w_gate, w_up, w_down
):
    row_count = tokens.shape[0]
    width_kv = KV_HEADS * HEAD_DIM
    group_size = HEADS // KV_HEADS
    score_scale = HEAD_DIM ** (-0.5)
    own_rows = D // RANKS
    down_rows = FF // RANKS
    late_rows = own_rows - ROWS
    main = RANKS * ROWS
    both_width, qkv_width = SHAPES[0][1], SHAPES[1][1]
    qkv_used = D + 2 * width_kv
    cuts = (0, both_width, both_width + qkv_width, both_width + qkv_width + LANES)

    def widen(v, width=LANES):
        return jnp.pad(v, ((0, 0), (0, width - v.shape[1])))

    def wide_dot(main_part, late_part, main_mat, late_mat):
        return jnp.dot(main_part, main_mat, preferred_element_type=jnp.float32) + jnp.dot(
            late_part, late_mat, preferred_element_type=jnp.float32
        )

    def back_dot(v, main_mat, late_mat):
        return right_dot(v, main_mat), right_dot(v, late_mat)

    def grad_dot(main_part, late_part, v):
        return (
            left_dot(main_part, v).astype(jnp.bfloat16),
            left_dot(late_part, v).astype(jnp.bfloat16),
        )

    own_both = jnp.concatenate([w.reshape(own_rows, FF) for w in (w_gate, w_up)], axis=1)
    own_qkv = jnp.concatenate(
        [w.reshape(own_rows, -1) for w in (w_query, w_key, w_value)]
        + [jnp.zeros((own_rows, qkv_width - qkv_used), jnp.bfloat16)],
        axis=1,
    )
    own_out = widen(w_output.reshape(own_rows, D))
    own_late = jnp.concatenate([own_both[ROWS:], own_qkv[ROWS:], own_out[ROWS:]], axis=1)
    slabs = gather_slabs(
        (
            own_both[:ROWS],
            own_qkv[:ROWS],
            widen(w_down.reshape(down_rows, D)),
            own_out[:ROWS],
            widen(own_late, LATE).reshape(ROWS, LANES),
        )
    )
    mat_both, mat_qkv, mat_down, mat_output = (
        slab.reshape(RANKS * slab.shape[1], slab.shape[2]) for slab in slabs[:4]
    )
    late = slabs[4].reshape(D - main, LATE)
    late_both, late_qkv, late_output = (late[:, low:high] for low, high in zip(cuts[:-1], cuts[1:]))
    spread = spread_matrix()

    def spread_rows(v):
        return (
            jnp.dot(v, spread[:, :main], preferred_element_type=jnp.float32).astype(jnp.bfloat16),
            jnp.dot(v, spread[:, main:], preferred_element_type=jnp.float32).astype(jnp.bfloat16),
        )

    def gather_back(pair, precision=lax.Precision.HIGHEST):
        return lax.dot_general(
            jnp.concatenate(pair, axis=1),
            spread.astype(pair[0].dtype),
            (((1,), (1,)), ((), ())),
            precision=precision,
            preferred_element_type=jnp.float32,
        )

    segment_row = segments[0]
    cosine_table, sine_table = rotary_tables(segment_row)
    inputs = tokens.astype(jnp.float32)
    normed_one, unit_one, inverse_one = norm_forward(inputs, norm_gains[0])
    normed_one = spread_rows(normed_one.astype(jnp.bfloat16))
    qkv = wide_dot(*normed_one, mat_qkv, late_qkv)
    queries = qkv[:, :D].reshape(row_count, HEADS, HEAD_DIM)
    key_rows = qkv[:, D : D + width_kv].reshape(row_count, KV_HEADS, HEAD_DIM)
    value_rows = qkv[:, D + width_kv : qkv_used].astype(jnp.bfloat16).reshape(row_count, KV_HEADS, HEAD_DIM)
    queries = rotate_pairs(queries, cosine_table, sine_table).astype(jnp.bfloat16)
    queries = queries.reshape(row_count, KV_HEADS, group_size, HEAD_DIM)
    key_rows = rotate_pairs(key_rows, cosine_table, sine_table).astype(jnp.bfloat16)
    pos = jnp.arange(row_count)
    allowed = (pos[None, :] <= pos[:, None]) & (segment_row[:, None] == segment_row[None, :])
    scores = (
        jnp.einsum("qkgd,tkd->kgqt", queries, key_rows, preferred_element_type=jnp.float32)
        * score_scale
    )
    scores = jnp.where(allowed[None, None], scores, NEGATIVE)
    exp_scores = jnp.exp(scores - jnp.max(scores, axis=-1, keepdims=True))
    probs = exp_scores / jnp.sum(exp_scores, axis=-1, keepdims=True)
    attention = probs.astype(jnp.bfloat16)
    mixed = jnp.einsum("kgqt,tkd->qkgd", attention, value_rows, preferred_element_type=jnp.float32)
    mixed = spread_rows(mixed.reshape(row_count, D).astype(jnp.bfloat16))
    residual = inputs + wide_dot(*mixed, mat_output, late_output)[:, :D]
    normed_two, unit_two, inverse_two = norm_forward(residual, norm_gains[1])
    normed_two = spread_rows(normed_two.astype(jnp.bfloat16))
    both = wide_dot(*normed_two, mat_both, late_both)
    gate_pre, up_pre = both[:, :FF], both[:, FF:]
    sigmoid_gate = jax.nn.sigmoid(gate_pre)
    activated = gate_pre * sigmoid_gate
    hidden = (activated * up_pre).astype(jnp.bfloat16)
    output = (
        residual + jnp.dot(hidden, mat_down, preferred_element_type=jnp.float32)[:, :D]
    ).astype(jnp.bfloat16)

    cotangent_wide = widen(cotangent)
    grad_wdown = left_dot(hidden, cotangent_wide).astype(jnp.bfloat16)
    grad_hidden = right_dot(cotangent_wide, mat_down)
    grad_gate = (
        grad_hidden * up_pre * sigmoid_gate * (1.0 + gate_pre * (1.0 - sigmoid_gate))
    ).astype(jnp.bfloat16)
    grad_up = (grad_hidden * activated).astype(jnp.bfloat16)
    grad_both = jnp.concatenate([grad_gate, grad_up], axis=1)
    grad_wboth, grad_late_both = grad_dot(*normed_two, grad_both)
    grad_normed_two = gather_back(back_dot(grad_both, mat_both, late_both))
    grad_from_norm, gain_two = norm_backward(grad_normed_two, unit_two, inverse_two, norm_gains[1])
    grad_residual = cotangent.astype(jnp.float32) + grad_from_norm
    grad_attn = grad_residual.astype(jnp.bfloat16)
    grad_attn_wide = widen(grad_attn)
    grad_woutput, grad_late_output = grad_dot(*mixed, grad_attn_wide)
    grad_mixed = tuple(
        v.astype(jnp.bfloat16) for v in back_dot(grad_attn_wide, mat_output, late_output)
    )
    grad_mixed = gather_back(grad_mixed, lax.Precision.DEFAULT).astype(jnp.bfloat16)
    grad_mixed = grad_mixed.reshape(row_count, KV_HEADS, group_size, HEAD_DIM)
    grad_probs = jnp.einsum(
        "qkgd,tkd->kgqt", grad_mixed, value_rows, preferred_element_type=jnp.float32
    )
    grad_values = jnp.einsum(
        "kgqt,qkgd->tkd", attention, grad_mixed, preferred_element_type=jnp.float32
    )
    row_inner = jnp.sum(probs * grad_probs, axis=-1, keepdims=True)
    grad_scores = (probs * (grad_probs - row_inner)).astype(jnp.bfloat16)
    grad_queries = (
        jnp.einsum("kgqt,tkd->qkgd", grad_scores, key_rows, preferred_element_type=jnp.float32)
        * score_scale
    ).reshape(row_count, HEADS, HEAD_DIM)
    grad_keys = (
        jnp.einsum("kgqt,qkgd->tkd", grad_scores, queries, preferred_element_type=jnp.float32)
        * score_scale
    )
    grad_queries = rotate_back(grad_queries, cosine_table, sine_table).reshape(row_count, D)
    grad_keys = rotate_back(grad_keys, cosine_table, sine_table).reshape(row_count, width_kv)
    grad_qkv = jnp.concatenate(
        [
            grad_queries.astype(jnp.bfloat16),
            grad_keys.astype(jnp.bfloat16),
            grad_values.reshape(row_count, width_kv).astype(jnp.bfloat16),
            jnp.zeros((row_count, qkv_width - qkv_used), jnp.bfloat16),
        ],
        axis=1,
    )
    grad_wqkv, grad_late_qkv = grad_dot(*normed_one, grad_qkv)
    grad_normed_one = gather_back(back_dot(grad_qkv, mat_qkv, late_qkv))
    grad_input_norm, gain_one = norm_backward(grad_normed_one, unit_one, inverse_one, norm_gains[0])
    input_grad = (grad_residual + grad_input_norm).astype(jnp.bfloat16)

    grad_late = widen(
        jnp.concatenate([grad_late_both, grad_late_qkv, grad_late_output], axis=1), LATE
    )
    grads = (grad_wboth, grad_wqkv, grad_wdown, grad_woutput, grad_late)
    gains = jnp.pad(jnp.stack([gain_one, gain_two]), ((0, 6), (0, LANES - D)))
    sum_both, sum_qkv, sum_down, sum_output, sum_late, sum_gains = scatter_slabs(
        [grad.reshape(RANKS, *shape) for grad, shape in zip(grads, SHAPES)], gains
    )
    sum_late = sum_late.reshape(late_rows, LATE)

    def whole(main_sum, low, high, start):
        return jnp.concatenate(
            [main_sum[:, low:high], sum_late[:, start + low : start + high]], axis=0
        ).reshape(-1)

    gate, up = whole(sum_both, 0, FF, 0), whole(sum_both, FF, 2 * FF, 0)
    query = whole(sum_qkv, 0, D, both_width)
    key = whole(sum_qkv, D, D + width_kv, both_width)
    value = whole(sum_qkv, D + width_kv, qkv_used, both_width)
    own_output = whole(sum_output, 0, D, cuts[2])
    return (
        output,
        input_grad,
        sum_gains[:2, :D],
        query,
        key,
        value,
        own_output,
        gate,
        up,
        sum_down[:, :D].reshape(-1),
    )


def solution(mesh):
    placed = (
        P("fsdp", None),
        P("fsdp", None),
        P("fsdp", None),
        P(),
        P("fsdp"),
        P("fsdp"),
        P("fsdp"),
        P("fsdp"),
        P("fsdp"),
        P("fsdp"),
        P("fsdp"),
    )
    return jax.shard_map(
        fast_body if mesh.shape["fsdp"] == RANKS else plain_body,
        mesh=mesh,
        in_specs=placed,
        out_specs=(
            P("fsdp", None),
            P("fsdp", None),
            P(),
            P("fsdp"),
            P("fsdp"),
            P("fsdp"),
            P("fsdp"),
            P("fsdp"),
            P("fsdp"),
            P("fsdp"),
        ),
        check_vma=False,
    )
```

```python
import functools
import math

import jax
import jax.numpy as jnp
from jax import lax
from jax.experimental import pallas as pl
from jax.experimental.pallas import tpu as pltpu
from jax.sharding import PartitionSpec as P

D = 576
FF = 1536
HEADS = 9
KV_HEADS = 3
HEAD_DIM = 64
DOCS = 3


EPSILON = 1e-05
THETA = 100000.0
NEGATIVE = -1e30


def rotary_tables(segment_row):
    length = segment_row.shape[0]
    positions = jnp.arange(length, dtype=jnp.int32)
    doc_ids = jnp.arange(DOCS, dtype=jnp.int32)
    starts = jnp.sum((segment_row[None, :] < doc_ids[:, None]).astype(jnp.int32), axis=1)
    member = (segment_row[:, None] == doc_ids[None, :]).astype(jnp.int32)
    offsets = positions - jnp.sum(member * starts[None, :], axis=1)
    frequency = jnp.exp(
        jnp.arange(0, HEAD_DIM, 2).astype(jnp.float32) * (-math.log(THETA) / HEAD_DIM)
    )
    angles = offsets.astype(jnp.float32)[:, None] * frequency[None, :]
    angles = jnp.concatenate([angles, angles], axis=1)
    return (jnp.cos(angles), jnp.sin(angles))


def rotate_pairs(vectors, cosine_table, sine_table):
    half_width = vectors.shape[-1] // 2
    turned = jnp.concatenate([-vectors[..., half_width:], vectors[..., :half_width]], axis=-1)
    return vectors * cosine_table[:, None, :] + turned * sine_table[:, None, :]


def rotate_back(gradient, cosine_table, sine_table):
    half_width = gradient.shape[-1] // 2
    scaled = gradient * sine_table[:, None, :]
    turned = jnp.concatenate([scaled[..., half_width:], -scaled[..., :half_width]], axis=-1)
    return gradient * cosine_table[:, None, :] + turned


def norm_forward(vectors, gain_row):
    inverse = lax.rsqrt(jnp.mean(vectors * vectors, axis=-1, keepdims=True) + EPSILON)
    unit_rows = vectors * inverse
    return (unit_rows * gain_row, unit_rows, inverse)


def norm_backward(upstream, unit_rows, inverse, gain_row):
    scaled = upstream * gain_row
    grad_in = inverse * (scaled - unit_rows * jnp.mean(scaled * unit_rows, axis=-1, keepdims=True))
    return (grad_in, jnp.sum(upstream * unit_rows, axis=0))


def left_dot(first, second):
    return lax.dot_general(
        first, second, (((0,), (0,)), ((), ())), preferred_element_type=jnp.float32
    )


def right_dot(first, second):
    return lax.dot_general(
        first, second, (((1,), (1,)), ((), ())), preferred_element_type=jnp.float32
    )


def attn_shapes(flat_list):
    width_kv = KV_HEADS * HEAD_DIM
    return (
        flat_list[0].reshape(D, D),
        flat_list[1].reshape(D, width_kv),
        flat_list[2].reshape(D, width_kv),
        flat_list[3].reshape(D, D),
    )


def mlp_shapes(flat_list):
    return (flat_list[0].reshape(D, FF), flat_list[1].reshape(D, FF), flat_list[2].reshape(FF, D))


def plain_body(
    tokens, segments, cotangent, norm_gains, w_query, w_key, w_value, w_output, w_gate, w_up, w_down
):
    row_count = tokens.shape[0]
    width_kv = KV_HEADS * HEAD_DIM
    group_size = HEADS // KV_HEADS
    score_scale = HEAD_DIM ** (-0.5)
    block_rows = min(512, row_count)
    segment_row = segments[0]
    cosine_table, sine_table = rotary_tables(segment_row)
    inputs = tokens.astype(jnp.float32)
    attn_flat = (
        lax.all_gather(w_query, "fsdp", axis=0, tiled=True),
        lax.all_gather(w_key, "fsdp", axis=0, tiled=True),
        lax.all_gather(w_value, "fsdp", axis=0, tiled=True),
        lax.all_gather(w_output, "fsdp", axis=0, tiled=True),
    )
    mat_query, mat_key, mat_value, mat_output = attn_shapes(attn_flat)
    normed_one, unit_one, inverse_one = norm_forward(inputs, norm_gains[0])
    normed_one = normed_one.astype(jnp.bfloat16)
    queries = jnp.dot(normed_one, mat_query, preferred_element_type=jnp.float32).reshape(
        row_count, HEADS, HEAD_DIM
    )
    key_rows = jnp.dot(normed_one, mat_key, preferred_element_type=jnp.float32).reshape(
        row_count, KV_HEADS, HEAD_DIM
    )
    value_rows = jnp.dot(normed_one, mat_value, preferred_element_type=jnp.float32).astype(
        jnp.bfloat16
    )
    value_rows = value_rows.reshape(row_count, KV_HEADS, HEAD_DIM)
    queries = rotate_pairs(queries, cosine_table, sine_table).astype(jnp.bfloat16)
    queries = queries.reshape(row_count, KV_HEADS, group_size, HEAD_DIM)
    key_rows = rotate_pairs(key_rows, cosine_table, sine_table).astype(jnp.bfloat16)

    def block_scores(block_start, key_end):
        query_pos = block_start + jnp.arange(block_rows)
        key_pos = jnp.arange(key_end)
        causal = key_pos[None, :] <= query_pos[:, None]
        same_doc = segment_row[:, None] == segment_row[None, :]
        scores = (
            jnp.einsum("qkgd,tkd->kgqt", queries, key_rows, preferred_element_type=jnp.float32)
            * score_scale
        )
        return jnp.where((causal & same_doc)[None, None], scores, NEGATIVE)

    block_start = 0
    key_end = block_start + block_rows
    scores = block_scores(block_start, key_end)
    row_peak = jnp.max(scores, axis=-1, keepdims=True)
    exp_scores = jnp.exp(scores - row_peak)
    row_total = jnp.sum(exp_scores, axis=-1, keepdims=True)
    attention = (exp_scores / row_total).astype(jnp.bfloat16)
    logsum_blocks = [row_peak + jnp.log(row_total)]
    mixed_blocks = jnp.einsum(
        "kgqt,tkd->qkgd", attention, value_rows, preferred_element_type=jnp.float32
    )
    mixed = mixed_blocks.reshape(row_count, D).astype(jnp.bfloat16)
    residual = inputs + jnp.dot(mixed, mat_output, preferred_element_type=jnp.float32)
    mlp_flat = (
        lax.all_gather(w_gate, "fsdp", axis=0, tiled=True),
        lax.all_gather(w_up, "fsdp", axis=0, tiled=True),
        lax.all_gather(w_down, "fsdp", axis=0, tiled=True),
    )
    mat_gate, mat_up, mat_down = mlp_shapes(mlp_flat)
    normed_two, unit_two, inverse_two = norm_forward(residual, norm_gains[1])
    normed_two = normed_two.astype(jnp.bfloat16)
    gate_pre = jnp.dot(normed_two, mat_gate, preferred_element_type=jnp.float32)
    up_pre = jnp.dot(normed_two, mat_up, preferred_element_type=jnp.float32)
    activated = jax.nn.silu(gate_pre)
    hidden = (activated * up_pre).astype(jnp.bfloat16)
    output = (residual + jnp.dot(hidden, mat_down, preferred_element_type=jnp.float32)).astype(
        jnp.bfloat16
    )
    mlp_flat = (
        lax.all_gather(w_gate, "fsdp", axis=0, tiled=True),
        lax.all_gather(w_up, "fsdp", axis=0, tiled=True),
        lax.all_gather(w_down, "fsdp", axis=0, tiled=True),
    )
    mat_gate, mat_up, mat_down = mlp_shapes(mlp_flat)
    grad_wdown = left_dot(hidden, cotangent)
    grad_hidden = right_dot(cotangent, mat_down)
    sigmoid_gate = jax.nn.sigmoid(gate_pre)
    grad_gate = (
        grad_hidden * up_pre * sigmoid_gate * (1.0 + gate_pre * (1.0 - sigmoid_gate))
    ).astype(jnp.bfloat16)
    grad_up = (grad_hidden * activated).astype(jnp.bfloat16)
    grad_wgate = left_dot(normed_two, grad_gate)
    grad_wup = left_dot(normed_two, grad_up)
    grad_normed_two = right_dot(grad_gate, mat_gate) + right_dot(grad_up, mat_up)
    grad_from_norm, gain_two = norm_backward(grad_normed_two, unit_two, inverse_two, norm_gains[1])
    grad_residual = cotangent.astype(jnp.float32) + grad_from_norm
    attn_flat = (
        lax.all_gather(w_query, "fsdp", axis=0, tiled=True),
        lax.all_gather(w_key, "fsdp", axis=0, tiled=True),
        lax.all_gather(w_value, "fsdp", axis=0, tiled=True),
        lax.all_gather(w_output, "fsdp", axis=0, tiled=True),
    )
    mat_query, mat_key, mat_value, mat_output = attn_shapes(attn_flat)
    grad_attn = grad_residual.astype(jnp.bfloat16)
    grad_woutput = left_dot(mixed, grad_attn)
    grad_mixed = right_dot(grad_attn, mat_output).astype(jnp.bfloat16)
    grad_mixed = grad_mixed.reshape(row_count, KV_HEADS, group_size, HEAD_DIM)
    grad_query_blocks = []
    grad_keys = jnp.zeros((row_count, KV_HEADS, HEAD_DIM), jnp.float32)
    grad_values = jnp.zeros((row_count, KV_HEADS, HEAD_DIM), jnp.float32)
    for block_index, block_start in enumerate(range(0, row_count, block_rows)):
        key_end = block_start + block_rows
        scores = block_scores(block_start, key_end)
        attention = jnp.exp(scores - logsum_blocks[block_index])
        grad_probs = jnp.einsum(
            "qkgd,tkd->kgqt", grad_mixed, value_rows, preferred_element_type=jnp.float32
        )
        grad_values = grad_values.at[:key_end].add(
            jnp.einsum(
                "kgqt,qkgd->tkd",
                attention.astype(jnp.bfloat16),
                grad_mixed,
                preferred_element_type=jnp.float32,
            )
        )
        row_inner = jnp.sum(attention * grad_probs, axis=-1, keepdims=True)
        grad_scores = (attention * (grad_probs - row_inner)).astype(jnp.bfloat16)
        grad_query_blocks.append(
            jnp.einsum("kgqt,tkd->qkgd", grad_scores, key_rows, preferred_element_type=jnp.float32)
            * score_scale
        )
        grad_keys = grad_keys.at[:key_end].add(
            jnp.einsum("kgqt,qkgd->tkd", grad_scores, queries, preferred_element_type=jnp.float32)
            * score_scale
        )
    grad_queries = grad_query_blocks[0].reshape(row_count, HEADS, HEAD_DIM)
    grad_queries = (
        rotate_back(grad_queries, cosine_table, sine_table)
        .reshape(row_count, D)
        .astype(jnp.bfloat16)
    )
    grad_keys = (
        rotate_back(grad_keys, cosine_table, sine_table)
        .reshape(row_count, width_kv)
        .astype(jnp.bfloat16)
    )
    grad_values = grad_values.reshape(row_count, width_kv).astype(jnp.bfloat16)
    grad_wquery = left_dot(normed_one, grad_queries)
    grad_wkey = left_dot(normed_one, grad_keys)
    grad_wvalue = left_dot(normed_one, grad_values)
    grad_normed_one = (
        right_dot(grad_queries, mat_query)
        + right_dot(grad_keys, mat_key)
        + right_dot(grad_values, mat_value)
    )
    grad_input_norm, gain_one = norm_backward(grad_normed_one, unit_one, inverse_one, norm_gains[0])
    input_grad = (grad_residual + grad_input_norm).astype(jnp.bfloat16)
    gain_one, gain_two = lax.psum((gain_one, gain_two), "fsdp")
    gain_grads = jnp.stack([gain_one, gain_two])
    shards = (
        lax.psum_scatter(grad_wquery.reshape(-1), "fsdp", scatter_dimension=0, tiled=True),
        lax.psum_scatter(grad_wkey.reshape(-1), "fsdp", scatter_dimension=0, tiled=True),
        lax.psum_scatter(grad_wvalue.reshape(-1), "fsdp", scatter_dimension=0, tiled=True),
        lax.psum_scatter(grad_woutput.reshape(-1), "fsdp", scatter_dimension=0, tiled=True),
        lax.psum_scatter(grad_wgate.reshape(-1), "fsdp", scatter_dimension=0, tiled=True),
        lax.psum_scatter(grad_wup.reshape(-1), "fsdp", scatter_dimension=0, tiled=True),
        lax.psum_scatter(grad_wdown.reshape(-1), "fsdp", scatter_dimension=0, tiled=True),
    )
    return (
        output,
        input_grad,
        gain_grads,
        shards[0],
        shards[1],
        shards[2],
        shards[3],
        shards[4],
        shards[5],
        shards[6],
    )


RANKS = 32
LAYERS = 4
ROWS = 16
LATE = 5120
LANES = 640
SHAPES = ((16, 3072), (16, 1024), (48, LANES), (16, LANES), (16, LANES))
PARTS = tuple(range(len(SHAPES)))
FIRST_X = (0, 3)
FIRST_Y = (1, 2, 4)
FIRST_Z = (0, 1, 2)
LAST_Z = (3, 4)
MESH = pl.DeviceIdType.MESH


def place():
    me = lax.axis_index("fsdp")
    return me, me // 8, me % 8, me % 2


def near_order(z):
    half = z // 2
    return (z, 1 - z + 4 * half, 2 - half, 3 - 3 * half)


def flip(index, bit):
    return index + bit - 2 * bit * ((index // bit) % 2)


def meet(me, z, bits):
    barrier = pltpu.get_barrier_semaphore()
    for bit in bits:
        pl.semaphore_signal(barrier, inc=1, device_id=(flip(me, bit),), device_id_type=MESH)

    @pl.when(z > 0)
    def _():
        pl.semaphore_signal(barrier, inc=1, device_id=(me - 8,), device_id_type=MESH)

    @pl.when(z < LAYERS - 1)
    def _():
        pl.semaphore_signal(barrier, inc=1, device_id=(me + 8,), device_id_type=MESH)

    pl.semaphore_wait(barrier, len(bits) + 1 + ((z + 1) // 2) % 2)


def gather_kernel(*refs):
    ins, outs = refs[: len(PARTS)], refs[len(PARTS) : 2 * len(PARTS)]
    own_sem, send_sem, recv_sem = refs[2 * len(PARTS) :]
    me, z, rest, core = place()

    def copy(kind, part, slot, target, own=False):
        return pltpu.make_async_remote_copy(
            src_ref=ins[part] if own else outs[part].at[slot],
            dst_ref=outs[part].at[slot],
            send_sem=send_sem.at[kind, part, slot],
            recv_sem=recv_sem.at[part, slot],
            device_id=(target,),
            device_id_type=MESH,
        )

    sends = []

    def send(kind, part, slot, target, own=False, when=None):
        sends.append((kind, part, slot, target, own, when))
        if when is None:
            copy(kind, part, slot, target, own).start()
        else:

            @pl.when(when)
            def _():
                copy(kind, part, slot, target, own).start()

    def arrive(part, slot):
        copy(0, part, slot, me).wait_recv()

    def along(slot, layer, own, parts, both=False):
        for part in parts:
            up, down = z < LAYERS - 1, z > 0
            if not both:
                up, down = (layer < z) & up, (layer > z) & down
            send(0, part, slot, me + 8, own, up)
            send(1, part, slot, me - 8, own, down)

    def around(slot, own, parts):
        for part in parts:
            send(2, part, slot, flip(me, 2), own)
        for part in parts[::-1]:
            send(3, part, slot, flip(me, 4), own)

    def share(slot, parts, own=False):
        for part in parts:
            send(4, part, slot, flip(me, 1), own)

    meet(me, z, (1, 2, 4))
    order = near_order(z)
    around(me, True, LAST_Z)
    along(me, z, True, FIRST_Z, True)
    around(me, True, FIRST_Z)
    along(me, z, True, LAST_Z, True)
    share(me, PARTS, True)
    for part in PARTS:
        pltpu.make_async_copy(ins[part], outs[part].at[me], own_sem.at[part]).start()

    def same(layer):
        slot = layer * 8 + rest
        for part in FIRST_Z:
            arrive(part, slot)
        along(slot, layer, False, FIRST_Z)
        around(slot, False, FIRST_Z)
        share(slot, FIRST_Z)

    def beside(layer, parts):
        slot = layer * 8 + rest
        by_x, by_y = flip(slot, 2), flip(slot, 4)
        for part in parts:
            if part in FIRST_X:
                arrive(part, by_x)
                send(3, part, by_x, flip(me, 4))
            else:
                arrive(part, by_y)
                send(2, part, by_y, flip(me, 2))
        for part in parts:
            arrive(part, by_y if part in FIRST_X else by_x)
        if parts is LAST_Z:
            along(by_x, layer, False, parts, True)
            along(by_y, layer, False, parts, True)
        share(by_x, parts)
        share(by_y, parts)

    def across(layer, parts):
        slot = flip(flip(layer * 8 + rest, 2), 4)
        for part in parts:
            arrive(part, slot)
        if parts is LAST_Z:
            along(slot, layer, False, parts, True)
        share(slot, parts)

    def line(layer):
        slot = layer * 8 + rest
        for at in (slot, flip(slot, 2), flip(slot, 4), flip(flip(slot, 2), 4)):
            for part in LAST_Z:
                arrive(part, at)
            along(at, layer, False, LAST_Z)
            share(at, LAST_Z)

    beside(z, LAST_Z)
    across(z, LAST_Z)
    for step in range(1, LAYERS):
        same(order[step])
        beside(order[step - 1], FIRST_Z)
        line(order[step])
    beside(order[LAYERS - 1], FIRST_Z)
    for step in range(LAYERS):
        across(order[step], FIRST_Z)
    for layer in range(LAYERS):
        for pair in range(4):
            for part in PARTS:
                arrive(part, layer * 8 + pair * 2 + 1 - core)
    for part in PARTS:
        pltpu.make_async_copy(ins[part], outs[part].at[me], own_sem.at[part]).wait()
    for kind, part, slot, target, own, when in sends:
        if when is None:
            copy(kind, part, slot, target, own).wait_send()
        else:

            @pl.when(when)
            def _(kind=kind, part=part, slot=slot, target=target, own=own):
                copy(kind, part, slot, target, own).wait_send()


def gather_slabs(slabs):
    count = len(PARTS)
    return pl.pallas_call(
        gather_kernel,
        out_shape=[jax.ShapeDtypeStruct((RANKS, *shape), jnp.bfloat16) for shape in SHAPES],
        in_specs=[pl.BlockSpec(memory_space=pl.ANY)] * count,
        out_specs=[pl.BlockSpec(memory_space=pl.ANY)] * count,
        scratch_shapes=[
            pltpu.SemaphoreType.DMA((count,)),
            pltpu.SemaphoreType.DMA((5, count, RANKS)),
            pltpu.SemaphoreType.DMA((count, RANKS)),
        ],
        compiler_params=pltpu.CompilerParams(collective_id=0, has_side_effects=True),
        name="gather_weights",
    )(*slabs)


def scatter_kernel(*refs):
    groups, at = [], 0
    for extra in (1, 1, 0, 0, 0, 0, 0):
        groups.append(refs[at : at + len(PARTS) + extra])
        at += len(PARTS) + extra
    ins, outs, owns, sibs, hops, diags, zs = groups
    gains_in, gains_out = ins[-1], outs[-1]
    (
        gain_mine, gain_got, own_sem, sib_send, sib_recv, hop_send, hop_recv, diag_send, diag_recv,
        z_send, z_recv, gain_send, gain_recv,
    ) = refs[at:]
    me, z, rest, core = place()
    order = near_order(z)[::-1]
    meet(me, z, (1, 2, 4, 16))

    def dest(layer, turn):
        slot = layer * 8 + rest
        if turn % 2:
            slot = flip(slot, 2)
        if turn // 2:
            slot = flip(slot, 4)
        return slot

    def own_copy(part, layer, turn):
        return pltpu.make_async_copy(
            ins[part].at[dest(layer, turn)], owns[part].at[turn, layer], own_sem.at[part, turn, layer]
        )

    def remote(src, dst, send_sem, recv_sem, target):
        return pltpu.make_async_remote_copy(
            src_ref=src, dst_ref=dst, send_sem=send_sem, recv_sem=recv_sem,
            device_id=(target,), device_id_type=MESH,
        )

    def sib_copy(part, layer, turn):
        return remote(
            ins[part].at[flip(dest(layer, turn), 1)], sibs[part].at[turn, layer],
            sib_send.at[part, turn, layer], sib_recv.at[part, turn, layer], flip(me, 1),
        )

    def diag_copy(part, layer):
        return remote(
            owns[part].at[3, layer], diags[part].at[layer],
            diag_send.at[part, layer], diag_recv.at[part, layer], flip(me, 2 if part in FIRST_X else 4),
        )

    def hop_copy(part, layer, turn):
        return remote(
            owns[part].at[turn, layer], hops[part].at[turn - 1, layer],
            hop_send.at[part, turn - 1, layer], hop_recv.at[part, turn - 1, layer],
            flip(me, 2 if turn == 1 else 4),
        )

    def z_copy(part, layer, way):
        return remote(
            owns[part].at[0, layer], zs[part].at[way, layer],
            z_send.at[part, way, layer], z_recv.at[part, way, layer], me + 8 if way == 0 else me - 8,
        )

    def base(part, layer, turn):
        own_copy(part, layer, turn).wait()
        sib_copy(part, layer, turn).wait_recv()
        return owns[part][turn, layer].astype(jnp.float32) + sibs[part][turn, layer].astype(jnp.float32)

    def gain_copy(stage):
        return remote(
            gain_mine.at[stage], gain_got.at[stage], gain_send.at[stage], gain_recv.at[stage],
            flip(me, 2**stage),
        )

    def gain_step(stage):
        gain_copy(stage - 1).wait_recv()
        gain_mine[stage] = gain_mine[stage - 1] + gain_got[stage - 1]
        if stage < 5:
            gain_copy(stage).start()

    for turn in (3, 1, 2, 0):
        for layer in order:
            for part in PARTS:
                sib_copy(part, layer, turn).start()
                own_copy(part, layer, turn).start()
    gain_mine[0] = gains_in[...]
    gain_copy(0).start()
    for layer in order:
        for part in PARTS:
            owns[part][3, layer] = base(part, layer, 3).astype(jnp.bfloat16)
            diag_copy(part, layer).start()
    gain_step(1)
    for layer in order:
        for turn, part, more in (
            *[(1, part, False) for part in FIRST_X],
            *[(2, part, False) for part in FIRST_Y],
            *[(1, part, True) for part in FIRST_Y],
            *[(2, part, True) for part in FIRST_X],
        ):
            total = base(part, layer, turn)
            if more:
                diag_copy(part, layer).wait_recv()
                total = total + diags[part][layer].astype(jnp.float32)
            owns[part][turn, layer] = total.astype(jnp.bfloat16)
            hop_copy(part, layer, turn).start()
        if layer is order[1]:
            gain_step(2)
    gain_step(3)

    def below(part, layer):
        z_copy(part, layer, 0).wait_recv()
        owns[part][0, layer] = (
            owns[part][0, layer].astype(jnp.float32) + zs[part][0, layer].astype(jnp.float32)
        ).astype(jnp.bfloat16)

    def above(part, layer):
        z_copy(part, layer, 1).wait_recv()
        owns[part][0, layer] = (
            owns[part][0, layer].astype(jnp.float32) + zs[part][1, layer].astype(jnp.float32)
        ).astype(jnp.bfloat16)

    for layer in order[:-1]:
        for part in PARTS:
            total = base(part, layer, 0)
            for turn in (1, 2):
                hop_copy(part, layer, turn).wait_recv()
                total = total + hops[part][turn - 1, layer].astype(jnp.float32)
            owns[part][0, layer] = total.astype(jnp.bfloat16)
            pl.when((layer > z) & (z > 0))(functools.partial(below, part, layer))
            pl.when((layer < z) & (z < LAYERS - 1))(functools.partial(above, part, layer))
            pl.when(layer > z)(lambda: z_copy(part, layer, 0).start())
            pl.when(layer < z)(lambda: z_copy(part, layer, 1).start())
    gain_step(4)
    for part in PARTS:
        total = base(part, z, 0)
        for turn in (1, 2):
            hop_copy(part, z, turn).wait_recv()
            total = total + hops[part][turn - 1, z].astype(jnp.float32)
        outs[part][...] = total

        @pl.when(z > 0)
        def _():
            z_copy(part, z, 0).wait_recv()
            outs[part][...] = outs[part][...] + zs[part][0, z].astype(jnp.float32)

        @pl.when(z < LAYERS - 1)
        def _():
            z_copy(part, z, 1).wait_recv()
            outs[part][...] = outs[part][...] + zs[part][1, z].astype(jnp.float32)

    gain_step(5)
    gains_out[...] = gain_mine[5]
    for stage in range(5):
        gain_copy(stage).wait_send()
    for part in PARTS:
        for layer in order:
            for turn in range(4):
                sib_copy(part, layer, turn).wait_send()
            diag_copy(part, layer).wait_send()
            for turn in (1, 2):
                hop_copy(part, layer, turn).wait_send()
        for layer in order[:-1]:
            pl.when(layer > z)(lambda: z_copy(part, layer, 0).wait_send())
            pl.when(layer < z)(lambda: z_copy(part, layer, 1).wait_send())


def scatter_slabs(slabs, gains):
    count = len(PARTS)
    vmem = pl.BlockSpec(memory_space=pltpu.VMEM)

    def buffers(*lead):
        return [pltpu.VMEM((*lead, *shape), jnp.bfloat16) for shape in SHAPES]

    def semaphores(*lead):
        return [pltpu.SemaphoreType.DMA((count, *lead))] * 2

    return pl.pallas_call(
        scatter_kernel,
        out_shape=[jax.ShapeDtypeStruct(shape, jnp.float32) for shape in (*SHAPES, gains.shape)],
        in_specs=[pl.BlockSpec(memory_space=pl.ANY)] * count + [vmem],
        out_specs=[vmem] * (count + 1),
        scratch_shapes=[
            *buffers(4, LAYERS),
            *buffers(4, LAYERS),
            *buffers(2, LAYERS),
            *buffers(LAYERS),
            *buffers(2, LAYERS),
            pltpu.VMEM((6, *gains.shape), jnp.float32),
            pltpu.VMEM((5, *gains.shape), jnp.float32),
            pltpu.SemaphoreType.DMA((count, 4, LAYERS)),
            *semaphores(4, LAYERS),
            *semaphores(2, LAYERS),
            *semaphores(LAYERS),
            *semaphores(2, LAYERS),
            *[pltpu.SemaphoreType.DMA((5,))] * 2,
        ],
        compiler_params=pltpu.CompilerParams(
            collective_id=1, has_side_effects=True, vmem_limit_bytes=40 << 20
        ),
        name="scatter_gradients",
    )(*slabs, gains)


def spread_matrix():
    rows = D // RANKS
    k = jnp.arange(D)
    main = k // ROWS * rows + k % ROWS
    late = k - RANKS * ROWS
    rest = late // (rows - ROWS) * rows + ROWS + late % (rows - ROWS)
    perm = jnp.where(k < RANKS * ROWS, main, rest)
    return (jnp.arange(D)[:, None] == perm[None, :]).astype(jnp.bfloat16)


def fast_body(
    tokens, segments, cotangent, norm_gains, w_query, w_key, w_value, w_output, w_gate, w_up, w_down
):
    row_count = tokens.shape[0]
    width_kv = KV_HEADS * HEAD_DIM
    group_size = HEADS // KV_HEADS
    score_scale = HEAD_DIM ** (-0.5)
    own_rows = D // RANKS
    down_rows = FF // RANKS
    late_rows = own_rows - ROWS
    main = RANKS * ROWS
    both_width, qkv_width = SHAPES[0][1], SHAPES[1][1]
    qkv_used = D + 2 * width_kv
    cuts = (0, both_width, both_width + qkv_width, both_width + qkv_width + LANES)

    def widen(v, width=LANES):
        return jnp.pad(v, ((0, 0), (0, width - v.shape[1])))

    def wide_dot(main_part, late_part, main_mat, late_mat):
        return jnp.dot(main_part, main_mat, preferred_element_type=jnp.float32) + jnp.dot(
            late_part, late_mat, preferred_element_type=jnp.float32
        )

    def back_dot(v, main_mat, late_mat):
        return right_dot(v, main_mat), right_dot(v, late_mat)

    def grad_dot(main_part, late_part, v):
        return (
            left_dot(main_part, v).astype(jnp.bfloat16),
            left_dot(late_part, v).astype(jnp.bfloat16),
        )

    own_both = jnp.concatenate([w.reshape(own_rows, FF) for w in (w_gate, w_up)], axis=1)
    own_qkv = jnp.concatenate(
        [w.reshape(own_rows, -1) for w in (w_query, w_key, w_value)]
        + [jnp.zeros((own_rows, qkv_width - qkv_used), jnp.bfloat16)],
        axis=1,
    )
    own_out = widen(w_output.reshape(own_rows, D))
    own_late = jnp.concatenate([own_both[ROWS:], own_qkv[ROWS:], own_out[ROWS:]], axis=1)
    slabs = gather_slabs(
        (
            own_both[:ROWS],
            own_qkv[:ROWS],
            widen(w_down.reshape(down_rows, D)),
            own_out[:ROWS],
            widen(own_late, LATE).reshape(ROWS, LANES),
        )
    )
    mat_both, mat_qkv, mat_down, mat_output = (
        slab.reshape(RANKS * slab.shape[1], slab.shape[2]) for slab in slabs[:4]
    )
    late = slabs[4].reshape(D - main, LATE)
    late_both, late_qkv, late_output = (late[:, low:high] for low, high in zip(cuts[:-1], cuts[1:]))
    spread = spread_matrix()

    def spread_rows(v):
        return (
            jnp.dot(v, spread[:, :main], preferred_element_type=jnp.float32).astype(jnp.bfloat16),
            jnp.dot(v, spread[:, main:], preferred_element_type=jnp.float32).astype(jnp.bfloat16),
        )

    def gather_back(pair, precision=lax.Precision.HIGHEST):
        return lax.dot_general(
            jnp.concatenate(pair, axis=1),
            spread.astype(pair[0].dtype),
            (((1,), (1,)), ((), ())),
            precision=precision,
            preferred_element_type=jnp.float32,
        )

    segment_row = segments[0]
    cosine_table, sine_table = rotary_tables(segment_row)
    inputs = tokens.astype(jnp.float32)
    normed_one, unit_one, inverse_one = norm_forward(inputs, norm_gains[0])
    normed_one = spread_rows(normed_one.astype(jnp.bfloat16))
    qkv = wide_dot(*normed_one, mat_qkv, late_qkv)
    queries = qkv[:, :D].reshape(row_count, HEADS, HEAD_DIM)
    key_rows = qkv[:, D : D + width_kv].reshape(row_count, KV_HEADS, HEAD_DIM)
    value_rows = qkv[:, D + width_kv : qkv_used].astype(jnp.bfloat16).reshape(row_count, KV_HEADS, HEAD_DIM)
    queries = rotate_pairs(queries, cosine_table, sine_table).astype(jnp.bfloat16)
    queries = queries.reshape(row_count, KV_HEADS, group_size, HEAD_DIM)
    key_rows = rotate_pairs(key_rows, cosine_table, sine_table).astype(jnp.bfloat16)
    pos = jnp.arange(row_count)
    allowed = (pos[None, :] <= pos[:, None]) & (segment_row[:, None] == segment_row[None, :])
    scores = (
        jnp.einsum("qkgd,tkd->kgqt", queries, key_rows, preferred_element_type=jnp.float32)
        * score_scale
    )
    scores = jnp.where(allowed[None, None], scores, NEGATIVE)
    exp_scores = jnp.exp(scores - jnp.max(scores, axis=-1, keepdims=True))
    probs = exp_scores / jnp.sum(exp_scores, axis=-1, keepdims=True)
    attention = probs.astype(jnp.bfloat16)
    mixed = jnp.einsum("kgqt,tkd->qkgd", attention, value_rows, preferred_element_type=jnp.float32)
    mixed = spread_rows(mixed.reshape(row_count, D).astype(jnp.bfloat16))
    residual = inputs + wide_dot(*mixed, mat_output, late_output)[:, :D]
    normed_two, unit_two, inverse_two = norm_forward(residual, norm_gains[1])
    normed_two = spread_rows(normed_two.astype(jnp.bfloat16))
    both = wide_dot(*normed_two, mat_both, late_both)
    gate_pre, up_pre = both[:, :FF], both[:, FF:]
    sigmoid_gate = jax.nn.sigmoid(gate_pre)
    activated = gate_pre * sigmoid_gate
    hidden = (activated * up_pre).astype(jnp.bfloat16)
    output = (
        residual + jnp.dot(hidden, mat_down, preferred_element_type=jnp.float32)[:, :D]
    ).astype(jnp.bfloat16)

    cotangent_wide = widen(cotangent)
    grad_wdown = left_dot(hidden, cotangent_wide).astype(jnp.bfloat16)
    grad_hidden = right_dot(cotangent_wide, mat_down)
    grad_gate = (
        grad_hidden * up_pre * sigmoid_gate * (1.0 + gate_pre * (1.0 - sigmoid_gate))
    ).astype(jnp.bfloat16)
    grad_up = (grad_hidden * activated).astype(jnp.bfloat16)
    grad_both = jnp.concatenate([grad_gate, grad_up], axis=1)
    grad_wboth, grad_late_both = grad_dot(*normed_two, grad_both)
    grad_normed_two = gather_back(back_dot(grad_both, mat_both, late_both))
    grad_from_norm, gain_two = norm_backward(grad_normed_two, unit_two, inverse_two, norm_gains[1])
    grad_residual = cotangent.astype(jnp.float32) + grad_from_norm
    grad_attn = grad_residual.astype(jnp.bfloat16)
    grad_attn_wide = widen(grad_attn)
    grad_woutput, grad_late_output = grad_dot(*mixed, grad_attn_wide)
    grad_mixed = tuple(
        v.astype(jnp.bfloat16) for v in back_dot(grad_attn_wide, mat_output, late_output)
    )
    grad_mixed = gather_back(grad_mixed, lax.Precision.DEFAULT).astype(jnp.bfloat16)
    grad_mixed = grad_mixed.reshape(row_count, KV_HEADS, group_size, HEAD_DIM)
    grad_probs = jnp.einsum(
        "qkgd,tkd->kgqt", grad_mixed, value_rows, preferred_element_type=jnp.float32
    )
    grad_values = jnp.einsum(
        "kgqt,qkgd->tkd", attention, grad_mixed, preferred_element_type=jnp.float32
    )
    row_inner = jnp.sum(probs * grad_probs, axis=-1, keepdims=True)
    grad_scores = (probs * (grad_probs - row_inner)).astype(jnp.bfloat16)
    grad_queries = (
        jnp.einsum("kgqt,tkd->qkgd", grad_scores, key_rows, preferred_element_type=jnp.float32)
        * score_scale
    ).reshape(row_count, HEADS, HEAD_DIM)
    grad_keys = (
        jnp.einsum("kgqt,qkgd->tkd", grad_scores, queries, preferred_element_type=jnp.float32)
        * score_scale
    )
    grad_queries = rotate_back(grad_queries, cosine_table, sine_table).reshape(row_count, D)
    grad_keys = rotate_back(grad_keys, cosine_table, sine_table).reshape(row_count, width_kv)
    grad_qkv = jnp.concatenate(
        [
            grad_queries.astype(jnp.bfloat16),
            grad_keys.astype(jnp.bfloat16),
            grad_values.reshape(row_count, width_kv).astype(jnp.bfloat16),
            jnp.zeros((row_count, qkv_width - qkv_used), jnp.bfloat16),
        ],
        axis=1,
    )
    grad_wqkv, grad_late_qkv = grad_dot(*normed_one, grad_qkv)
    grad_normed_one = gather_back(back_dot(grad_qkv, mat_qkv, late_qkv))
    grad_input_norm, gain_one = norm_backward(grad_normed_one, unit_one, inverse_one, norm_gains[0])
    input_grad = (grad_residual + grad_input_norm).astype(jnp.bfloat16)

    grad_late = widen(
        jnp.concatenate([grad_late_both, grad_late_qkv, grad_late_output], axis=1), LATE
    )
    grads = (grad_wboth, grad_wqkv, grad_wdown, grad_woutput, grad_late)
    gains = jnp.pad(jnp.stack([gain_one, gain_two]), ((0, 6), (0, LANES - D)))
    sum_both, sum_qkv, sum_down, sum_output, sum_late, sum_gains = scatter_slabs(
        [grad.reshape(RANKS, *shape) for grad, shape in zip(grads, SHAPES)], gains
    )
    sum_late = sum_late.reshape(late_rows, LATE)

    def whole(main_sum, low, high, start):
        return jnp.concatenate(
            [main_sum[:, low:high], sum_late[:, start + low : start + high]], axis=0
        ).reshape(-1)

    gate, up = whole(sum_both, 0, FF, 0), whole(sum_both, FF, 2 * FF, 0)
    query = whole(sum_qkv, 0, D, both_width)
    key = whole(sum_qkv, D, D + width_kv, both_width)
    value = whole(sum_qkv, D + width_kv, qkv_used, both_width)
    own_output = whole(sum_output, 0, D, cuts[2])
    return (
        output,
        input_grad,
        sum_gains[:2, :D],
        query,
        key,
        value,
        own_output,
        gate,
        up,
        sum_down[:, :D].reshape(-1),
    )


def solution(mesh):
    placed = (
        P("fsdp", None),
        P("fsdp", None),
        P("fsdp", None),
        P(),
        P("fsdp"),
        P("fsdp"),
        P("fsdp"),
        P("fsdp"),
        P("fsdp"),
        P("fsdp"),
        P("fsdp"),
    )
    return jax.shard_map(
        fast_body if mesh.shape["fsdp"] == RANKS else plain_body,
        mesh=mesh,
        in_specs=placed,
        out_specs=(
            P("fsdp", None),
            P("fsdp", None),
            P(),
            P("fsdp"),
            P("fsdp"),
            P("fsdp"),
            P("fsdp"),
            P("fsdp"),
            P("fsdp"),
            P("fsdp"),
        ),
        check_vma=False,
    )
```
